256 devices in a mesh: group: 32 (over z_hi, x, core), tp: 8 (over z_lo, y).
Axes of the slice: x: 4, y: 4, z: 8 (z_hi: 4, z_lo: 2; z = z_hi * 2 + z_lo), core: 2. Of those that a mesh axis runs over, the one named last changes fastest.
Arguments:
- queries: bfloat16 [16384, 4096], P('group', 'tp'), may hold values from -5 to 5
- fresh_kv: bfloat16 [16384, 2048], P('group', 'tp'), may hold values from -4.5 to 4.5
- page_pool: bfloat16 [3840, 64, 2048], P('group', None, 'tp'), may hold values from -5 to 5
- out_weight: bfloat16 [4096, 8192], P('tp'), may hold values from -0.5 to 0.5
- request_row: int32 [256], replicated, may hold values from 0 to 2047, as said below
- request_len: int32 [256], replicated, may hold values from 129 to 384
- request_pages: int32 [256, 6], replicated, may hold values from 24 to 119, as said below
- resident_len: int32 [2048], replicated, may hold values from 0 to 64, as said below
- prefix_len: int32 [16], replicated, may hold values from 64 to 1536
Outputs:
- hidden: bfloat16 [16384, 8192], P(('group', 'tp'))
The draws below stay inside these ranges and needn't reach their ends.
Inputs may be any that keep to these rules, and one draw needn't show every extreme that they name: `request_row`: all distinct; each prefill group sends exactly one request to each decode group (the group is request_row // 128). `request_pages`: the rows of one prefill group's requests hold distinct pages, all from 24 on. `resident_len`: exactly 0 on the rows that receive a request, 1 or more on the others.
All inputs are finite; a program needn't handle non-finite values.
Results may differ from the reference program's by a relative error of at most 0.022.
Values may be sent and summed in bfloat16 or wider, within the bound.
No kernel may reach another device: no remote copies, remote signals or barrier semaphores. Data moves between devices by JAX's collectives and lax.ppermute only.
A program may use at most 192 MiB of HBM per device.

```python
import math
import jax
import jax.numpy as jnp
from jax import lax

D = 8192
KVH = 8
HD = 128
QH = 32
P_SIZE = 64
POS = 4
PREF = 24
MAXP = 6
ROWS = 512
NPRE = 16
NDEC = 16
HAND = 16
NREQ = 256
NPOOL = 120
DROWS = 128
ALLROWS = 16384
ALLPAGES = 3840
N_GROUP = 32
N_TP = 8


def handover_plan(key):
    key = jax.random.fold_in(key, 11)
    key_dest, key_row, key_pages, key_within, key_table, key_resident = jax.random.split(key, 6)

    def shuffle_groups(sub_key):
        return jax.random.permutation(sub_key, NDEC)

    def shuffle_rows(sub_key):
        return jax.random.permutation(sub_key, DROWS)

    def shuffle_pages(sub_key):
        return jax.random.permutation(sub_key, HAND * MAXP)
    dest_group = jax.vmap(shuffle_groups)(jax.random.split(key_dest, NPRE)).reshape(NREQ).astype(jnp.int32)
    row_order = jax.vmap(shuffle_rows)(jax.random.split(key_row, NDEC)).astype(jnp.int32)
    source = jnp.arange(NREQ, dtype=jnp.int32) // HAND
    request_row = dest_group * DROWS + row_order[dest_group, source]
    pages_used = jax.random.randint(key_pages, (NREQ,), MAXP // 2, MAXP + 1)
    within = jax.random.randint(key_within, (NREQ,), 1, P_SIZE + 1)
    request_len = (pages_used - 1) * P_SIZE + within
    request_len = request_len.at[0].set(MAXP * P_SIZE).at[1].set((MAXP // 2 - 1) * P_SIZE + 1)
    tables = jax.vmap(shuffle_pages)(jax.random.split(key_table, NPRE)).astype(jnp.int32)
    request_pages = (tables + PREF).reshape(NREQ, MAXP)
    arrived = jnp.zeros((NDEC * DROWS,), jnp.int32).at[request_row].set(1)
    resident = jax.random.randint(key_resident, (NDEC * DROWS,), 1, P_SIZE + 1)
    resident_len = jnp.where(arrived > 0, 0, resident).at[row_order[0, DROWS - 1]].set(P_SIZE)
    return (request_row, request_len.astype(jnp.int32), request_pages, resident_len.astype(jnp.int32))


def draw_request_row(key, part):
    return handover_plan(key)[0]


def draw_request_len(key, part):
    return handover_plan(key)[1]


def draw_request_pages(key, part):
    return handover_plan(key)[2]


def draw_resident_len(key, part):
    return handover_plan(key)[3]


def draw_prefix_len(key, part):
    key = jax.random.fold_in(key, 5)
    drawn = jax.random.randint(key, (NPRE,), P_SIZE, PREF * P_SIZE + 1)
    return drawn.at[0].set(PREF * P_SIZE).at[1].set(P_SIZE).astype(jnp.int32)


def draw_queries(key, part):
    key = jax.random.fold_in(key, 3)
    key_base = jax.random.fold_in(key, 0)
    drawn = jnp.clip(jax.random.normal(key_base, (ALLROWS, QH * HD), jnp.float32), -4.5, 4.5)
    return drawn.astype(jnp.bfloat16)


def draw_page_pool(key, part):
    key = jax.random.fold_in(key, 7)
    key_base = jax.random.fold_in(key, 0)
    pool_shape = (ALLPAGES, P_SIZE, KVH, 2, HD)
    drawn = jnp.clip(jax.random.normal(key_base, pool_shape, jnp.float32), -4.5, 4.5)
    return drawn.reshape(ALLPAGES, P_SIZE, 2 * KVH * HD).astype(jnp.bfloat16)


def block_levels(key, extent, pieces, low, high):
    def one(dim, blocks):
        steps = jax.random.uniform(jax.random.fold_in(jax.random.fold_in(key, 6), dim), (blocks,), jnp.float32, low / len(pieces), high / len(pieces))
        return jnp.repeat(jnp.exp(steps), extent[dim] // blocks).reshape((-1,) + (1,) * (len(extent) - dim - 1))

    level = one(*pieces[0])
    for cut in pieces[1:]:
        level = level * one(*cut)
    return level


def scatter_about(stream_key, shape, width, most, cuts=(), held_as=jnp.bfloat16):
    loudness = block_levels(stream_key, shape, cuts, -0.22, 0.18) if cuts else 1.0
    entries = jax.random.normal(stream_key, shape, jnp.float32) * width * loudness
    return jnp.minimum(jnp.maximum(entries, -most), most).astype(held_as)


def setup_inputs(seed: int = 0) -> dict:
    splits = jax.random.split(jax.random.key(seed), 10)
    queries = draw_queries(jax.random.fold_in(splits[9], 71), 0)
    fresh_kv = scatter_about(splits[1], (ALLROWS, 2 * KVH * HD), 1.0, 4.5, ((0, 32), (1, 8)))
    page_pool = draw_page_pool(jax.random.fold_in(splits[9], 71), 0)
    out_weight = scatter_about(splits[3], (QH * HD, D), HD ** -0.5, 0.5, ((0, 8),))
    request_row = draw_request_row(jax.random.fold_in(splits[9], 71), 0)
    request_len = draw_request_len(jax.random.fold_in(splits[9], 71), 0)
    request_pages = draw_request_pages(jax.random.fold_in(splits[9], 71), 0)
    resident_len = draw_resident_len(jax.random.fold_in(splits[9], 71), 0)
    prefix_len = draw_prefix_len(jax.random.fold_in(splits[9], 71), 0)
    return {"queries": queries, "fresh_kv": fresh_kv, "page_pool": page_pool, "out_weight": out_weight, "request_row": request_row, "request_len": request_len, "request_pages": request_pages, "resident_len": resident_len, "prefix_len": prefix_len}


def attend(query_in, key_in, value_in, allowed):
    scores = jnp.einsum('brkgd,bskd->bkgrs', query_in.astype(jnp.float32), key_in.astype(jnp.float32)) / math.sqrt(HD)
    scores = jnp.where(allowed[:, None, None, :, :], scores, -1e+30)
    weights = jax.nn.softmax(scores, axis=-1).astype(jnp.bfloat16)
    mixed = jnp.einsum('bkgrs,bskd->brkgd', weights.astype(jnp.float32), value_in.astype(jnp.float32))
    return mixed.astype(jnp.bfloat16)

def reference(queries, fresh_kv, page_pool, out_weight, request_row, request_len, request_pages, resident_len, prefix_len):
    ratio = QH // KVH
    query_all = queries.reshape(N_GROUP, ROWS, KVH, ratio, HD)
    fresh_all = fresh_kv.reshape(N_GROUP, ROWS, KVH, 2, HD)
    pool_all = page_pool.reshape(N_GROUP, NPOOL, P_SIZE, KVH, 2, HD)
    flat_pool = page_pool.reshape(N_GROUP * NPOOL, P_SIZE, KVH, 2, HD)
    prefix_tokens = PREF * P_SIZE
    context_tokens = MAXP * P_SIZE

    def prefill(prefill_id):
        prefix = pool_all[prefill_id][:PREF].reshape(prefix_tokens, KVH, 2, HD)
        all_keys = jnp.concatenate([prefix, fresh_all[prefill_id]], axis=0)
        key_pos = jnp.arange(prefix_tokens + ROWS, dtype=jnp.int32)[None, :]
        row_pos = jnp.arange(ROWS, dtype=jnp.int32)[:, None]
        allowed = jnp.where(key_pos < prefix_tokens, key_pos < prefix_len[prefill_id], key_pos - prefix_tokens <= row_pos)
        return attend(query_all[prefill_id][None], all_keys[None, :, :, 0], all_keys[None, :, :, 1], allowed[None])[0]
    row_request = jnp.full((NDEC * DROWS,), -1, jnp.int32).at[request_row].set(jnp.arange(NREQ, dtype=jnp.int32))

    def decode(decode_id):
        group_id = NPRE + decode_id
        local_req = lax.dynamic_slice_in_dim(row_request, decode_id * DROWS, DROWS)
        arrived = local_req >= 0
        request = jnp.maximum(local_req, 0)
        row_ids = jnp.arange(DROWS, dtype=jnp.int32)
        remote = (request // HAND)[:, None] * NPOOL + request_pages[request]
        resident_pages = group_id * NPOOL + jnp.broadcast_to((row_ids % NPOOL)[:, None], (DROWS, MAXP))
        page_ids = jnp.where(arrived[:, None], remote, resident_pages)
        length = jnp.where(arrived, request_len[request], lax.dynamic_slice_in_dim(resident_len, decode_id * DROWS, DROWS))
        context = flat_pool[page_ids].reshape(DROWS, context_tokens, KVH, 2, HD)
        new_keys = fresh_all[group_id].reshape(DROWS, POS, KVH, 2, HD)
        all_keys = jnp.concatenate([context, new_keys], axis=1)
        key_pos = jnp.arange(context_tokens + POS, dtype=jnp.int32)[None, None, :]
        step_pos = jnp.arange(POS, dtype=jnp.int32)[None, :, None]
        allowed = jnp.where(key_pos < context_tokens, key_pos < length[:, None, None], key_pos - context_tokens <= step_pos)
        query_rows = query_all[group_id].reshape(DROWS, POS, KVH, ratio, HD)
        mixed = attend(query_rows, all_keys[:, :, :, 0], all_keys[:, :, :, 1], allowed)
        return mixed.reshape(ROWS, KVH, ratio, HD)
    prefill_out = lax.map(prefill, jnp.arange(NPRE, dtype=jnp.int32))
    decode_out = lax.map(decode, jnp.arange(NDEC, dtype=jnp.int32))
    attention = jnp.concatenate([prefill_out, decode_out], axis=0).reshape(N_GROUP * ROWS, N_TP, QH * HD // N_TP)
    weight_blocks = out_weight.reshape(N_TP, QH * HD // N_TP, D)

    def add_block(block_id, summed):
        partial_value = jnp.dot(attention[:, block_id], weight_blocks[block_id], preferred_element_type=jnp.float32).astype(jnp.bfloat16)
        partial_value = lax.optimization_barrier(partial_value)
        return summed + partial_value.astype(jnp.float32)
    summed = lax.fori_loop(0, N_TP, add_block, jnp.zeros((N_GROUP * ROWS, D), jnp.float32))
    return summed.astype(jnp.bfloat16)
```

```python
import functools
import math

import jax
import jax.numpy as jnp
from jax import lax
from jax.experimental import pallas as pl
from jax.experimental.pallas import tpu as pltpu
from jax.sharding import PartitionSpec as P

HD = 128
POS = 4
PREF = 24
HEADS = 4
NEG = -1e30
SCALE2 = math.log2(math.e) / math.sqrt(HD)
BF = jnp.bfloat16
F32 = jnp.float32


def nt_dot(a, b):
    return lax.dot_general(a, b, (((1,), (1,)), ((), ())), preferred_element_type=F32)


def nn_dot(a, b):
    return jnp.dot(a, b, preferred_element_type=F32)


def soft_mix(pieces):
    top = functools.reduce(
        jnp.maximum, [jnp.max(s, axis=-1, keepdims=True) for s, _ in pieces]
    )
    total = 0.0
    mixed = 0.0
    for s, v in pieces:
        p = jnp.exp2((s - top) * SCALE2)
        total = total + jnp.sum(p, axis=-1, keepdims=True)
        mixed = mixed + nn_dot(p.astype(BF), v)
    return (mixed / total).astype(BF)


def local_kernel(info, queries, fresh, pool, lens, out, *, rows, page_len, pool_pages):
    is_prefill, my_y, my_z, prefix = info[0], info[1], info[2], info[3]

    def place(row):
        dest = row // 64
        dist_y = lax.rem(lax.rem(dest, 4) - my_y + 4, 4)
        dist_z = jnp.abs(dest // 4 - my_z)
        return pl.multiple_of((dist_y * 2 + dist_z) * 64 + lax.rem(row, 64), 32)

    prefix_tokens = PREF * page_len

    @pl.when(is_prefill == 1)
    def _():
        span = 64

        def chunk(i, carry):
            row = pl.multiple_of(i * span, span)
            where_to = place(row)
            key_p = pool[0:PREF, :, 0:HD].reshape(prefix_tokens, HD)
            val_p = pool[0:PREF, :, HD : 2 * HD].reshape(prefix_tokens, HD)
            ok_p = lax.broadcasted_iota(jnp.int32, (1, prefix_tokens), 1) < prefix
            row_id = lax.broadcasted_iota(jnp.int32, (span, rows), 0) + row
            ok_f = lax.broadcasted_iota(jnp.int32, (span, rows), 1) <= row_id
            for h in range(HEADS):
                q = queries[pl.ds(row, span), h * HD : (h + 1) * HD]
                s_p = jnp.where(ok_p, nt_dot(q, key_p), NEG)
                s_f = jnp.where(ok_f, nt_dot(q, fresh[:, 0:HD]), NEG)
                o = soft_mix([(s_p, val_p), (s_f, fresh[:, HD : 2 * HD])])
                out[pl.ds(where_to, span), h * HD : (h + 1) * HD] = o
            return carry

        lax.fori_loop(0, rows // span, chunk, 0)

    @pl.when(is_prefill == 0)
    def _():
        each = 8
        span = each * POS
        stack = span * HEADS
        width = each * page_len
        row_id = lax.rem(lax.broadcasted_iota(jnp.int32, (stack, width), 0), span) // POS
        same = lax.broadcasted_iota(jnp.int32, (stack, width), 1) // page_len == row_id
        f_row = lax.rem(lax.broadcasted_iota(jnp.int32, (stack, span), 0), span)
        f_col = lax.broadcasted_iota(jnp.int32, (stack, span), 1)
        f_ok = jnp.logical_and(f_col // POS == f_row // POS, f_col <= f_row)

        def chunk(i, carry):
            row = pl.multiple_of(i * span, span)
            first = lax.rem(i * each, pool_pages)
            where_to = place(row)
            q = jnp.concatenate(
                [queries[pl.ds(row, span), h * HD : (h + 1) * HD] for h in range(HEADS)], axis=0
            )
            key_r = pool[pl.ds(first, each), :, 0:HD].reshape(width, HD)
            val_r = pool[pl.ds(first, each), :, HD : 2 * HD].reshape(width, HD)
            ok = jnp.logical_and(same, lens[pl.ds(i, 1), :] > 0)
            s_r = jnp.where(ok, nt_dot(q, key_r), NEG)
            s_f = jnp.where(f_ok, nt_dot(q, fresh[pl.ds(row, span), 0:HD]), NEG)
            o = soft_mix([(s_r, val_r), (s_f, fresh[pl.ds(row, span), HD : 2 * HD])])
            for h in range(HEADS):
                out[pl.ds(where_to, span), h * HD : (h + 1) * HD] = o[h * span : (h + 1) * span]
            return carry

        lax.fori_loop(0, rows // span, chunk, 0)


def handed_kernel(info, pages, lengths, pool, sent, out, *, count, most, page_len):
    @pl.when(info[0] == 1)
    def _():
        stack = POS * HEADS
        width = most * page_len
        col = lax.broadcasted_iota(jnp.int32, (1, width), 1)
        f_row = lax.broadcasted_iota(jnp.int32, (stack, 8), 0) // HEADS
        f_col = lax.broadcasted_iota(jnp.int32, (stack, 8), 1)
        f_ok = f_col <= f_row

        def one(i, carry):
            q = sent[i, 0:stack, :]
            new = sent[i, stack : stack + 16, :].astype(F32)
            key_n = new[0:8].astype(BF)
            val_n = new[8:16].astype(BF)
            ids = [pages[i, n] for n in range(most)]
            key_c = jnp.concatenate([pool[p, :, 0:HD] for p in ids], axis=0)
            val_c = jnp.concatenate([pool[p, :, HD : 2 * HD] for p in ids], axis=0)
            s_c = jnp.where(col < lengths[i], nt_dot(q, key_c), NEG)
            s_n = jnp.where(f_ok, nt_dot(q, key_n), NEG)
            out[i] = soft_mix([(s_c, val_c), (s_n, val_n)])
            return carry

        lax.fori_loop(0, count, one, 0, unroll=4)


def add(*terms):
    total = terms[0].astype(F32)
    for term in terms[1:]:
        total = total + term.astype(F32)
    return total.astype(BF)


def on_device(
    queries,
    fresh_kv,
    page_pool,
    out_weight,
    request_row,
    request_len,
    request_pages,
    resident_len,
    prefix_len,
):
    group_count = lax.axis_size("group")
    tp_count = lax.axis_size("tp")
    half = group_count // 2
    group = lax.axis_index("group")
    tp = lax.axis_index("tp")
    my_y, my_z = tp % 4, tp // 4
    rows = queries.shape[0]
    pool_pages, page_len, _ = page_pool.shape
    most = request_pages.shape[1]
    decode_rows = rows // POS
    is_prefill = group < half
    peer = group % half

    def y_step(x, step):
        return lax.ppermute(x, "tp", [(t, t // 4 * 4 + (t + step) % 4) for t in range(tp_count)])

    def z_swap(x):
        return lax.ppermute(x, "tp", [(t, (t + 4) % tp_count) for t in range(tp_count)])

    row_table = request_row.reshape(half, half)
    dest = row_table // decode_rows
    to_me = dest == peer
    my_rows = jnp.sum(jnp.where(to_me, row_table % decode_rows, 0), axis=1)
    own_dest = lax.dynamic_index_in_dim(dest, peer, 0, keepdims=False)
    match = own_dest[None, :] == jnp.arange(half, dtype=jnp.int32)[:, None]
    own_pages = lax.dynamic_index_in_dim(
        request_pages.reshape(half, half, most), peer, 0, keepdims=False
    )
    own_len = lax.dynamic_index_in_dim(request_len.reshape(half, half), peer, 0, keepdims=False)
    pages = jnp.sum(jnp.where(match[:, :, None], own_pages[None], 0), axis=1)
    lengths = jnp.sum(jnp.where(match, own_len[None], 0), axis=1)

    wanted = (my_rows[:, None] * POS + jnp.arange(POS, dtype=jnp.int32)[None, :]).reshape(-1)
    pick = (wanted[:, None] == jnp.arange(rows, dtype=jnp.int32)[None, :]).astype(BF)
    picked_q = jnp.dot(pick, queries, preferred_element_type=F32).astype(BF)
    picked_f = jnp.dot(pick, fresh_kv, preferred_element_type=F32).astype(BF)
    picked_f = picked_f.reshape(half, POS, 2, HD)
    fill = jnp.zeros((half, 8 - POS, HD), BF)
    parcel = jnp.concatenate(
        [
            picked_q.reshape(half, POS * HEADS, HD),
            picked_f[:, :, 0],
            fill,
            picked_f[:, :, 1],
            fill,
        ],
        axis=1,
    )
    outgoing = jnp.concatenate([parcel, parcel], axis=0)
    sent = lax.all_to_all(outgoing, "group", split_axis=0, concat_axis=0, tiled=True)[half:]

    info = jnp.stack(
        [
            is_prefill.astype(jnp.int32),
            my_y.astype(jnp.int32),
            my_z.astype(jnp.int32),
            prefix_len[peer],
        ]
    )
    my_resident = lax.dynamic_slice_in_dim(resident_len, peer * decode_rows, decode_rows)
    seen = jnp.arange(page_len, dtype=jnp.int32)[None, :] < my_resident[:, None]
    seen = seen.astype(F32).reshape(decode_rows // 8, 8 * page_len)
    smem = pl.BlockSpec(memory_space=pltpu.SMEM)
    vmem = pl.BlockSpec(memory_space=pltpu.VMEM)
    params = pltpu.CompilerParams(vmem_limit_bytes=40 * 1024 * 1024)
    local = pl.pallas_call(
        functools.partial(local_kernel, rows=rows, page_len=page_len, pool_pages=pool_pages),
        out_shape=jax.ShapeDtypeStruct((rows, HEADS * HD), BF),
        in_specs=[smem, vmem, vmem, vmem, vmem],
        out_specs=vmem,
        compiler_params=params,
        cost_estimate=pl.CostEstimate(
            flops=4 * 2048 * 2048 * 128, bytes_accessed=5 << 20, transcendentals=1 << 22
        ),
        name="local_attention",
    )(info, queries, fresh_kv, page_pool, seen)
    handed = pl.pallas_call(
        functools.partial(handed_kernel, count=half, most=most, page_len=page_len),
        out_shape=jax.ShapeDtypeStruct((half, POS * HEADS, HD), BF),
        in_specs=[smem, smem, smem, vmem, vmem],
        out_specs=vmem,
        compiler_params=params,
        name="handed_attention",
    )(info, pages, lengths, page_pool, sent)

    back = jnp.concatenate([handed, handed], axis=0)
    back = lax.all_to_all(back, "group", split_axis=0, concat_axis=0, tiled=True)[:half]
    back = back.reshape(half * POS, HEADS * HD)

    dest_t = wanted // 64
    spot = (((dest_t % 4 - my_y) % 4) * 2 + jnp.abs(dest_t // 4 - my_z)) * 64 + wanted % 64
    put = jnp.logical_and(
        jnp.arange(rows, dtype=jnp.int32)[:, None] == spot[None, :], jnp.logical_not(is_prefill)
    )
    moved = jnp.dot(put.astype(BF), back, preferred_element_type=F32).astype(BF)
    attention = jnp.where(jnp.any(put, axis=1)[:, None], moved, local)

    def along_y(blocks):
        mid = blocks[0].shape[-1] // 2
        far_r = y_step(blocks[2][..., :mid], 1)
        far_l = y_step(blocks[2][..., mid:], -1)
        right = jnp.concatenate([add(blocks[1][..., :mid], far_r), blocks[1][..., mid:]], -1)
        left = jnp.concatenate([blocks[3][..., :mid], add(blocks[3][..., mid:], far_l)], -1)
        return add(blocks[0], y_step(right, 1), y_step(left, -1))

    share = rows // tp_count
    done = []
    begin = 0
    for first, wide in (("y", 4608), ("z", 3584)):
        part = jnp.dot(
            attention, out_weight[:, begin : begin + wide], preferred_element_type=F32
        ).astype(BF)
        part = part.reshape(4, 2, share, wide)
        begin += wide
        if first == "y":
            mine = along_y([part[d] for d in range(4)])
            done.append(add(mine[0], z_swap(mine[1])))
        else:
            mine = add(part[:, 0], z_swap(part[:, 1]))
            done.append(along_y([mine[d] for d in range(4)]))
    return jnp.concatenate(done, axis=-1)


def solution(mesh):
    in_specs = (
        P("group", "tp"),
        P("group", "tp"),
        P("group", None, "tp"),
        P("tp", None),
        P(),
        P(),
        P(),
        P(),
        P(),
    )
    out_specs = P(("group", "tp"), None)
    return jax.shard_map(
        on_device, mesh=mesh, in_specs=in_specs, out_specs=out_specs, check_vma=False
    )
```

```python
import functools
import math

import jax
import jax.numpy as jnp
from jax import lax
from jax.experimental import pallas as pl
from jax.experimental.pallas import tpu as pltpu
from jax.sharding import PartitionSpec as P

HD = 128
POS = 4
PREF = 24
HEADS = 4
NEG = -1e30
LARGE = 54
SMALL = 54
COLS = (768, 4608, 2816)
LATE = 2816
FRONT = 54
SCALE2 = math.log2(math.e) / math.sqrt(HD)
BF = jnp.bfloat16
F32 = jnp.float32


def nt_dot(a, b):
    return lax.dot_general(a, b, (((1,), (1,)), ((), ())), preferred_element_type=F32)


def nn_dot(a, b):
    return jnp.dot(a, b, preferred_element_type=F32)


def soft_mix(pieces):
    top = functools.reduce(
        jnp.maximum, [jnp.max(s, axis=-1, keepdims=True) for s, _ in pieces]
    )
    total = 0.0
    mixed = 0.0
    for s, v in pieces:
        p = jnp.exp2((s - top) * SCALE2)
        total = total + jnp.sum(p, axis=-1, keepdims=True)
        mixed = mixed + nn_dot(p.astype(BF), v)
    return (mixed / total).astype(BF)


def wanted_rows(table, group, half, decode_rows):
    slots = half * HEADS * POS
    peer = lax.rem(group, half)
    slot = lax.broadcasted_iota(jnp.int32, (slots, half * half), 0)
    request = lax.broadcasted_iota(jnp.int32, (slots, half * half), 1)
    row = table[...]
    mine = jnp.logical_and(
        request // half == slot // (HEADS * POS), row // decode_rows == peer
    )
    first = jnp.sum(jnp.where(mine, lax.rem(row, decode_rows) * POS, 0), axis=1, keepdims=True)
    return first + lax.rem(lax.broadcasted_iota(jnp.int32, (slots, 1), 0), POS)


def pick_kernel(table, queries, fresh, out, *, half, decode_rows):
    rows = queries.shape[0]
    slots = half * HEADS * POS
    want = wanted_rows(table, lax.axis_index("group"), half, decode_rows)
    pick = (want == lax.broadcasted_iota(jnp.int32, (slots, rows), 1)).astype(F32).astype(BF)
    head = lax.rem(lax.broadcasted_iota(jnp.int32, (slots, HD), 0) // POS, HEADS)
    got_q = nn_dot(pick, queries[...])
    got_f = nn_dot(pick, fresh[...])
    one_q = got_q[:, 0:HD]
    for h in range(1, HEADS):
        one_q = jnp.where(head == h, got_q[:, h * HD : (h + 1) * HD], one_q)
    one_f = jnp.where(head == 0, got_f[:, 0:HD], got_f[:, HD : 2 * HD])
    one_f = jnp.where(head < 2, one_f, 0.0)
    for n in range(2):
        out[n * slots : (n + 1) * slots, 0:HD] = one_q.astype(BF)
        out[n * slots : (n + 1) * slots, HD : 2 * HD] = one_f.astype(BF)


def stacked(ref, row, span):
    return jnp.concatenate(
        [ref[pl.ds(row, span), h * HD : (h + 1) * HD] for h in range(HEADS)], axis=0
    )


def fresh_mask(span):
    row = lax.rem(lax.broadcasted_iota(jnp.int32, (span * HEADS, span), 0), span)
    col = lax.broadcasted_iota(jnp.int32, (span * HEADS, span), 1)
    return jnp.logical_and(col // POS == row // POS, col <= row)


def turn(dist):
    return jnp.where(dist == 0, 3, jnp.where(dist == 1, 1, jnp.where(dist == 2, 0, 2)))


def local_kernel(prefix_len, resident_len, queries, fresh, pool, out, held, sems, *, half, part):
    group = lax.axis_index("group")
    tp = lax.axis_index("tp")
    peer = lax.rem(group, half)
    my_y = lax.rem(tp, 4)
    rows = queries.shape[0]
    pool_pages, page_len, _ = pool.shape
    each = 8
    parts = pool_pages // each

    def fetch(n):
        return pltpu.make_async_copy(
            pool.at[pl.ds(n * each, each)], held.at[pl.ds(n * each, each)], sems.at[n]
        )

    def place(row):
        dist_y = lax.rem(lax.rem(row // 64, 4) - my_y + 4, 4)
        return pl.multiple_of(turn(dist_y) * 64 + lax.rem(row, 64), 32)

    @pl.when(group < half)
    def _():
        prefix_tokens = PREF * page_len
        for n in range(PREF // each):
            fetch(n).start()
        for n in range(PREF // each):
            fetch(n).wait()
        prefix = prefix_len[peer]
        span = 64
        stack = span * HEADS
        ok_p = lax.broadcasted_iota(jnp.int32, (1, prefix_tokens), 1) < prefix
        row_id = lax.rem(lax.broadcasted_iota(jnp.int32, (stack, rows), 0), span)
        ahead = lax.broadcasted_iota(jnp.int32, (stack, rows), 1) - row_id

        def chunk(i, carry):
            row = pl.multiple_of(i * span, span)
            where_to = place(row)
            q = stacked(queries, row, span)
            key_p = held[0:PREF, :, 0:HD].reshape(prefix_tokens, HD)
            val_p = held[0:PREF, :, HD : 2 * HD].reshape(prefix_tokens, HD)
            s_p = jnp.where(ok_p, nt_dot(q, key_p), NEG)
            s_f = jnp.where(ahead <= row, nt_dot(q, fresh[:, 0:HD]), NEG)
            o = soft_mix([(s_p, val_p), (s_f, fresh[:, HD : 2 * HD])])
            for h in range(HEADS):
                out[pl.ds(where_to, span), h * HD : (h + 1) * HD] = o[h * span : (h + 1) * span]
            return carry

        lax.fori_loop(part * (rows // span // 2), (part + 1) * (rows // span // 2), chunk, 0)

    @pl.when(group >= half)
    def _():
        steps = rows // POS // each
        mine = range(part * (steps // 2), min((part + 1) * (steps // 2), parts))
        if part == 1:
            fetch(0).start()
        for n in mine:
            fetch(n).start()
        if part == 1:
            fetch(0).wait()
        span = each * POS
        stack = span * HEADS
        width = each * page_len
        decode_rows = rows // POS
        row_id = lax.rem(lax.broadcasted_iota(jnp.int32, (stack, width), 0), span) // POS
        col = lax.broadcasted_iota(jnp.int32, (stack, width), 1)
        same = col // page_len == row_id
        slot = lax.broadcasted_iota(jnp.int32, (1, width), 1)
        f_ok = fresh_mask(span)

        def chunk(i, carry):
            @pl.when(i < parts)
            def _():
                fetch(i).wait()

            row = pl.multiple_of(i * span, span)
            first = lax.rem(i, parts) * each
            where_to = place(row)
            q = stacked(queries, row, span)
            key_r = held[pl.ds(first, each), :, 0:HD].reshape(width, HD)
            val_r = held[pl.ds(first, each), :, HD : 2 * HD].reshape(width, HD)
            length = jnp.zeros((1, width), jnp.int32)
            for e in range(each):
                length = jnp.where(
                    slot // page_len == e, resident_len[peer * decode_rows + i * each + e], length
                )
            seen = lax.rem(slot, page_len) < length
            s_r = jnp.where(jnp.logical_and(same, seen), nt_dot(q, key_r), NEG)
            s_f = jnp.where(f_ok, nt_dot(q, fresh[pl.ds(row, span), 0:HD]), NEG)
            o = soft_mix([(s_r, val_r), (s_f, fresh[pl.ds(row, span), HD : 2 * HD])])
            for h in range(HEADS):
                out[pl.ds(where_to, span), h * HD : (h + 1) * HD] = o[h * span : (h + 1) * span]
            return carry

        lax.fori_loop(part * (rows // span // 2), (part + 1) * (rows // span // 2), chunk, 0)


def handed_kernel(
    table, lengths, pages, all_pages, sent, out, slots, pool, sems, *, half, decode_rows
):
    group = lax.axis_index("group")
    most = pages.shape[0]
    page_len = pool.shape[1]
    each = 4
    stack = HEADS * POS
    span = each * stack
    width = each * most * page_len

    @pl.when(group >= half)
    def _():
        out[...] = jnp.zeros_like(out)

    @pl.when(group < half)
    def _():
        parts = sems.shape[0]
        each_part = pool.shape[0] // parts

        def fetch(n):
            at = pl.ds(n * each_part, each_part)
            return pltpu.make_async_copy(all_pages.at[at], pool.at[at], sems.at[n])

        for n in range(parts):
            fetch(n).start()
        for i in range(half):
            slots[table[group * half + i] // decode_rows] = group * half + i
        row_id = lax.broadcasted_iota(jnp.int32, (span, width), 0) // stack
        col = lax.broadcasted_iota(jnp.int32, (span, width), 1)
        same = col // (most * page_len) == row_id
        slot = lax.broadcasted_iota(jnp.int32, (1, width), 1)
        f_row = lax.broadcasted_iota(jnp.int32, (span, span), 0)
        f_col = lax.broadcasted_iota(jnp.int32, (span, span), 1)
        f_ok = jnp.logical_and(
            f_row // stack == f_col // stack, lax.rem(f_col, stack) <= lax.rem(f_row, POS)
        )
        for n in range(parts):
            fetch(n).wait()
        for b in range(half // each):
            length = jnp.zeros((1, width), jnp.int32)
            ids = []
            for e in range(each):
                request = slots[b * each + e]
                ids += [pages[n, request] for n in range(most)]
                length = jnp.where(slot // (most * page_len) == e, lengths[request], length)
            seen = lax.rem(slot, most * page_len) < length
            new = sent[(half // each + b) * span : (half // each + b + 1) * span, :]
            q = new[:, 0:HD]
            key_n = new[:, HD : 2 * HD]
            val_n = pltpu.roll(key_n.astype(F32), span - POS, 0).astype(BF)
            key_c = jnp.concatenate([pool[n, :, 0:HD] for n in ids], axis=0)
            val_c = jnp.concatenate([pool[n, :, HD : 2 * HD] for n in ids], axis=0)
            s_c = jnp.where(jnp.logical_and(same, seen), nt_dot(q, key_c), NEG)
            s_n = jnp.where(f_ok, nt_dot(q, key_n), NEG)
            o = soft_mix([(s_c, val_c), (s_n, val_n)])
            for n in range(2):
                out[(n * half // each + b) * span : (n * half // each + b + 1) * span, :] = o


def front_kernel(
    table, first, second, back, weight, x13, x0, near, far, y_r, y_l, a1, held, sems, *, half, decode_rows
):
    group = lax.axis_index("group")
    tp = lax.axis_index("tp")
    my_z = tp // 4
    rows, wide = first.shape
    slots = half * HEADS * POS
    count, _, part = held.shape

    def fetch(n):
        begin = (n + 1) * part if n < count - 1 else 0
        return pltpu.make_async_copy(
            weight.at[:, pl.ds(begin, part)], held.at[n], sems.at[n]
        )

    for n in range(count):
        fetch(n).start()

    @pl.when(my_z == 0)
    def _():
        near[...] = first[...]
        far[...] = second[...]

    @pl.when(my_z == 1)
    def _():
        near[...] = second[...]
        far[...] = first[...]

    @pl.when(group >= half)
    def _():
        want = wanted_rows(table, group, half, decode_rows)
        dest = want // 64
        dist_y = lax.rem(lax.rem(dest, 4) - lax.rem(tp, 4) + 4, 4)
        spot = turn(dist_y) * 64 + lax.rem(want, 64)
        dist_z = jnp.abs(dest // 4 - my_z)
        here = lax.broadcasted_iota(jnp.int32, (slots, rows), 1)
        head = lax.rem(lax.broadcasted_iota(jnp.int32, (slots, HD), 0) // POS, HEADS)
        came = back[0:slots, :].astype(F32)
        came = [jnp.where(head == h, came, 0.0).astype(BF) for h in range(HEADS)]
        for dist, out in ((0, near), (1, far)):
            put = jnp.logical_and(spot == here, dist_z == dist).astype(F32).astype(BF)

            def spread(x):
                return lax.dot_general(
                    put, x, (((0,), (0,)), ((), ())), preferred_element_type=F32
                )

            hit = spread(jnp.ones((slots, HD), BF)) > 0.5
            for h in range(HEADS):
                at = slice(h * HD, (h + 1) * HD)
                out[:, at] = jnp.where(hit, spread(came[h]), out[:, at].astype(F32)).astype(BF)

    share = rows // 4
    x2 = jnp.concatenate([near[0:share], far[0:share]], axis=0)
    for n in range(count - 1):
        fetch(n).wait()
        piece = nn_dot(x2, held[n]).astype(BF)
        out, at = (y_r, n) if n < (count - 1) // 2 else (y_l, n - (count - 1) // 2)
        out[:, at * part : (at + 1) * part] = piece
    fetch(count - 1).wait()
    a1[...] = nn_dot(far[...], held[count - 1]).astype(BF)
    for n, d in enumerate((1, 2)):
        x13[2 * n * share : (2 * n + 1) * share] = near[d * share : (d + 1) * share]
        x13[(2 * n + 1) * share : (2 * n + 2) * share] = far[d * share : (d + 1) * share]
    x0[0:share] = near[3 * share :]
    x0[share:] = far[3 * share :]


def add(*terms):
    total = terms[0].astype(F32)
    for term in terms[1:]:
        total = total + term.astype(F32)
    return total.astype(BF)


def on_device(
    queries,
    fresh_kv,
    page_pool,
    out_weight,
    request_row,
    request_len,
    request_pages,
    resident_len,
    prefix_len,
):
    half = lax.axis_size("group") // 2
    tp_count = lax.axis_size("tp")
    rows, wide = queries.shape
    kv_wide = fresh_kv.shape[1]
    pool_pages, page_len, _ = page_pool.shape
    most = request_pages.shape[1]
    decode_rows = rows // POS
    slots = half * HEADS * POS
    smem = pl.BlockSpec(memory_space=pltpu.SMEM)
    vmem = pl.BlockSpec(memory_space=pltpu.VMEM)
    anywhere = pl.BlockSpec(memory_space=pl.ANY)
    large = pltpu.CompilerParams(vmem_limit_bytes=LARGE * 1024 * 1024)
    small = pltpu.CompilerParams(vmem_limit_bytes=SMALL * 1024 * 1024)

    def y_step(x, step):
        return lax.ppermute(x, "tp", [(t, t // 4 * 4 + (t + step) % 4) for t in range(tp_count)])

    def z_swap(x):
        return lax.ppermute(x, "tp", [(t, (t + 4) % tp_count) for t in range(tp_count)])

    table = request_row.reshape(1, half * half)
    parcel = pl.pallas_call(
        functools.partial(pick_kernel, half=half, decode_rows=decode_rows),
        out_shape=jax.ShapeDtypeStruct((2 * slots, kv_wide), BF),
        in_specs=[vmem] * 3,
        out_specs=vmem,
        compiler_params=large,
        name="pick_rows",
    )(table, queries, fresh_kv)
    sent = lax.all_to_all(parcel, "group", split_axis=0, concat_axis=0, tiled=True)

    def attend_half(part):
        return pl.pallas_call(
            functools.partial(local_kernel, half=half, part=part),
            out_shape=jax.ShapeDtypeStruct((rows // 2, wide), BF),
            in_specs=[smem, smem, vmem, vmem, anywhere],
            out_specs=vmem,
            scratch_shapes=[
                pltpu.VMEM(page_pool.shape, BF),
                pltpu.SemaphoreType.DMA((pool_pages // 8,)),
            ],
            compiler_params=large,
            cost_estimate=pl.CostEstimate(
                flops=8 * 2048 * 2048 * 128, bytes_accessed=5 << 20, transcendentals=1 << 21
            ),
            name="local_attention",
        )(prefix_len, resident_len, queries, fresh_kv, page_pool)

    first = attend_half(0)
    sent, first = lax.optimization_barrier((sent, first))
    handed = pl.pallas_call(
        functools.partial(handed_kernel, half=half, decode_rows=decode_rows),
        out_shape=jax.ShapeDtypeStruct((2 * slots, HD), BF),
        in_specs=[smem, smem, smem, anywhere, vmem],
        out_specs=vmem,
        scratch_shapes=[
            pltpu.SMEM((half,), jnp.int32),
            pltpu.VMEM(page_pool.shape, BF),
            pltpu.SemaphoreType.DMA((pool_pages // 8,)),
        ],
        compiler_params=small,
        name="handed_attention",
    )(request_row, request_len, request_pages.T, page_pool, sent)
    back = lax.all_to_all(handed, "group", split_axis=0, concat_axis=0, tiled=True)
    second = attend_half(1)
    share = rows // tp_count
    cols_a, cols_y, cols_b = COLS
    pieces = cols_y // cols_a + 1

    def made(*shape):
        return jax.ShapeDtypeStruct(shape, BF)

    x13, x0, near, far, y2_r, y2_l, a1 = pl.pallas_call(
        functools.partial(front_kernel, half=half, decode_rows=decode_rows),
        out_shape=(
            made(4 * share, wide),
            made(2 * share, wide),
            made(4 * share, wide),
            made(4 * share, wide),
            made(2 * share, cols_y // 2),
            made(2 * share, cols_y // 2),
            made(4 * share, cols_a),
        ),
        in_specs=[vmem] * 4 + [anywhere],
        out_specs=(vmem,) * 7,
        scratch_shapes=[
            pltpu.VMEM((pieces, wide, cols_a), BF),
            pltpu.SemaphoreType.DMA((pieces,)),
        ],
        compiler_params=pltpu.CompilerParams(vmem_limit_bytes=FRONT * 1024 * 1024),
        name="front_products",
    )(table, first, second, back, out_weight)

    cuts = {"a": (0, cols_a), "y": (cols_a, cols_a + cols_y), "b": (cols_a + cols_y, sum(COLS))}

    def blocks(x):
        return x.reshape(-1, share, x.shape[1])

    def products(given, names):
        parts = []
        for name in names:
            begin, end = cuts[name[0]]
            part = jnp.dot(
                given[name], out_weight[:, begin:end], preferred_element_type=F32
            ).astype(BF)
            part, given = lax.optimization_barrier((part, given))
            parts.append(blocks(part))
        return parts, given

    def start_far(far):
        mid = far.shape[-1] // 2
        return y_step(far[..., :mid], 1), y_step(far[..., mid:], -1)

    def start_near(next_r, next_l, far_r, far_l):
        mid = far_r.shape[-1]
        right = jnp.concatenate([add(next_r[..., :mid], far_r), next_r[..., mid:]], -1)
        left = jnp.concatenate([next_l[..., :mid], add(next_l[..., mid:], far_l)], -1)
        return y_step(right, 1), y_step(left, -1)

    far_y = y_step(blocks(y2_r), 1), y_step(blocks(y2_l), -1)
    come_a = z_swap(blocks(a1))
    given = {"y13": x13, "b1": far, "a0": near, "y0": x0, "b0": near}
    (y13, b1), given = products(given, ("y13", "b1"))
    far_y, come_a, given, y13, b1 = lax.optimization_barrier((far_y, come_a, given, y13, b1))

    near_y = start_near(y13[0:2], y13[2:4], *far_y)
    come_b = z_swap(b1)
    (a0, y0, b0), given = products(given, ("a0", "y0", "b0"))
    mine_a = add(a0, come_a)
    far_a = start_far(mine_a[0])
    near_y, come_b, far_a, y0, b0 = lax.optimization_barrier((near_y, come_b, far_a, y0, b0))

    mine_y = add(y0, *near_y)
    soon = cols_y - LATE
    come_y = z_swap(mine_y[1][:, :soon])
    mine_b = add(b0, come_b)
    far_b = start_far(mine_b[0])
    near_a = start_near(mine_a[1], mine_a[2], *far_a)
    come_y, far_b, near_a, mine_y, mine_b = lax.optimization_barrier(
        (come_y, far_b, near_a, mine_y, mine_b)
    )

    late_y = z_swap(mine_y[1][:, soon:])
    near_b = start_near(mine_b[1], mine_b[2], *far_b)
    return jnp.concatenate(
        [
            add(mine_a[3], *near_a),
            add(mine_y[0][:, :soon], come_y),
            add(mine_y[0][:, soon:], late_y),
            add(mine_b[3], *near_b),
        ],
        axis=-1,
    )


def solution(mesh):
    in_specs = (
        P("group", "tp"),
        P("group", "tp"),
        P("group", None, "tp"),
        P("tp", None),
        P(),
        P(),
        P(),
        P(),
        P(),
    )
    out_specs = P(("group", "tp"), None)
    return jax.shard_map(
        on_device, mesh=mesh, in_specs=in_specs, out_specs=out_specs, check_vma=False
    )
```

```python
import functools
import math

import jax
import jax.numpy as jnp
from jax import lax
from jax.experimental import pallas as pl
from jax.experimental.pallas import tpu as pltpu
from jax.sharding import PartitionSpec as P

HD = 128
POS = 4
PREF = 24
HEADS = 4
NEG = -1e30
COLS_Y = 4608
PIECE = 256
EARLY = 1024
FIRST = 5
LIMIT = 54
LESS = 52
SCALE2 = math.log2(math.e) / math.sqrt(HD)
BF = jnp.bfloat16
F32 = jnp.float32


def nt_dot(a, b):
    return lax.dot_general(a, b, (((1,), (1,)), ((), ())), preferred_element_type=F32)


def nn_dot(a, b):
    return jnp.dot(a, b, preferred_element_type=F32)


def soft_mix(pieces):
    top = functools.reduce(
        jnp.maximum, [jnp.max(s, axis=-1, keepdims=True) for s, _ in pieces]
    )
    total = 0.0
    mixed = 0.0
    for s, v in pieces:
        p = jnp.exp2((s - top) * SCALE2)
        total = total + jnp.sum(p, axis=-1, keepdims=True)
        mixed = mixed + nn_dot(p.astype(BF), v)
    return (mixed / total).astype(BF)


def wanted_rows(table, group, half, decode_rows):
    slots = half * HEADS * POS
    peer = lax.rem(group, half)
    slot = lax.broadcasted_iota(jnp.int32, (slots, half * half), 0)
    request = lax.broadcasted_iota(jnp.int32, (slots, half * half), 1)
    row = table[...]
    mine = jnp.logical_and(
        request // half == slot // (HEADS * POS), row // decode_rows == peer
    )
    first = jnp.sum(jnp.where(mine, lax.rem(row, decode_rows) * POS, 0), axis=1, keepdims=True)
    return first + lax.rem(lax.broadcasted_iota(jnp.int32, (slots, 1), 0), POS)


def load(pairs, sems):
    copies = [pltpu.make_async_copy(a, b, sems.at[n]) for n, (a, b) in enumerate(pairs)]
    for copy in copies:
        copy.start()
    return copies


def pick_kernel(table, all_q, all_f, out, queries, fresh, sems, *, half, decode_rows):
    copies = load([(all_q, queries), (all_f, fresh)], sems)
    rows = queries.shape[0]
    slots = half * HEADS * POS
    want = wanted_rows(table, lax.axis_index("group"), half, decode_rows)
    pick = (want == lax.broadcasted_iota(jnp.int32, (slots, rows), 1)).astype(F32).astype(BF)
    head = lax.rem(lax.broadcasted_iota(jnp.int32, (slots, HD), 0) // POS, HEADS)
    for copy in copies:
        copy.wait()
    got_q = nn_dot(pick, queries[...])
    got_f = nn_dot(pick, fresh[...])
    one_q = got_q[:, 0:HD]
    for h in range(1, HEADS):
        one_q = jnp.where(head == h, got_q[:, h * HD : (h + 1) * HD], one_q)
    one_f = jnp.where(head == 0, got_f[:, 0:HD], got_f[:, HD : 2 * HD])
    one_f = jnp.where(head < 2, one_f, 0.0)
    for n in range(2):
        out[n * slots : (n + 1) * slots, 0:HD] = one_q.astype(BF)
        out[n * slots : (n + 1) * slots, HD : 2 * HD] = one_f.astype(BF)


def stacked(ref, row, span):
    return jnp.concatenate(
        [ref[pl.ds(row, span), h * HD : (h + 1) * HD] for h in range(HEADS)], axis=0
    )


def fresh_mask(span):
    row = lax.rem(lax.broadcasted_iota(jnp.int32, (span * HEADS, span), 0), span)
    col = lax.broadcasted_iota(jnp.int32, (span * HEADS, span), 1)
    return jnp.logical_and(col // POS == row // POS, col <= row)


def local_kernel(
    prefix_len, resident_len, *refs, half, decode_rows, part, cut
):
    if part == 0:
        table, pages, all_q, all_f, pool, out, gathered, *scratch = refs
    else:
        all_q, all_f, pool, out, *scratch = refs
    queries, fresh, held, io_sems, sems, *more = scratch
    copies = load([(all_q, queries), (all_f, fresh)], io_sems)

    group = lax.axis_index("group")
    peer = lax.rem(group, half)
    rows = queries.shape[0]
    begin, end = (0, cut) if part == 0 else (cut, rows)
    pool_pages, page_len, _ = pool.shape
    each = 8
    parts = pool_pages // each

    def fetch(n):
        return pltpu.make_async_copy(
            pool.at[pl.ds(n * each, each)], held.at[pl.ds(n * each, each)], sems.at[n]
        )

    def side_copies():
        if part == 1:
            return []
        most = pages.shape[0]
        return [
            pltpu.make_async_copy(
                pool.at[pages[n, more[1][d]]], gathered.at[d * most + n], more[0].at[d, n]
            )
            for d in range(half)
            for n in range(most)
        ]

    @pl.when(group < half)
    def _():
        prefix_tokens = PREF * page_len
        for n in range(PREF // each):
            fetch(n).start()
        if part == 0:
            for i in range(half):
                more[1][table[group * half + i] // decode_rows] = group * half + i
        for copy in side_copies():
            copy.start()
        for copy in copies:
            copy.wait()
        for n in range(PREF // each):
            fetch(n).wait()
        prefix = prefix_len[peer]
        span = 64
        stack = span * HEADS
        ok_p = lax.broadcasted_iota(jnp.int32, (1, prefix_tokens), 1) < prefix
        row_id = lax.rem(lax.broadcasted_iota(jnp.int32, (stack, rows), 0), span)
        ahead = lax.broadcasted_iota(jnp.int32, (stack, rows), 1) - row_id

        def chunk(i, carry):
            row = pl.multiple_of(i * span, span)
            q = stacked(queries, row, span)
            key_p = held[0:PREF, :, 0:HD].reshape(prefix_tokens, HD)
            val_p = held[0:PREF, :, HD : 2 * HD].reshape(prefix_tokens, HD)
            s_p = jnp.where(ok_p, nt_dot(q, key_p), NEG)
            s_f = jnp.where(ahead <= row, nt_dot(q, fresh[:, 0:HD]), NEG)
            o = soft_mix([(s_p, val_p), (s_f, fresh[:, HD : 2 * HD])])
            for h in range(HEADS):
                out[pl.ds(row - begin, span), h * HD : (h + 1) * HD] = o[h * span : (h + 1) * span]
            return carry

        lax.fori_loop(begin // span, end // span, chunk, 0)
        for copy in side_copies():
            copy.wait()

    @pl.when(group >= half)
    def _():
        span = each * POS
        if part == 1:
            fetch(0).start()
        for n in range(begin // span, min(end // span, parts)):
            fetch(n).start()
        if part == 1:
            fetch(0).wait()
        for copy in copies:
            copy.wait()
        stack = span * HEADS
        width = each * page_len
        row_id = lax.rem(lax.broadcasted_iota(jnp.int32, (stack, width), 0), span) // POS
        col = lax.broadcasted_iota(jnp.int32, (stack, width), 1)
        same = col // page_len == row_id
        slot = lax.broadcasted_iota(jnp.int32, (1, width), 1)
        f_ok = fresh_mask(span)

        def chunk(i, carry):
            @pl.when(i < parts)
            def _():
                fetch(i).wait()

            row = pl.multiple_of(i * span, span)
            first = lax.rem(i, parts) * each
            q = stacked(queries, row, span)
            key_r = held[pl.ds(first, each), :, 0:HD].reshape(width, HD)
            val_r = held[pl.ds(first, each), :, HD : 2 * HD].reshape(width, HD)
            length = jnp.zeros((1, width), jnp.int32)
            for e in range(each):
                length = jnp.where(
                    slot // page_len == e, resident_len[peer * decode_rows + i * each + e], length
                )
            seen = lax.rem(slot, page_len) < length
            s_r = jnp.where(jnp.logical_and(same, seen), nt_dot(q, key_r), NEG)
            s_f = jnp.where(f_ok, nt_dot(q, fresh[pl.ds(row, span), 0:HD]), NEG)
            o = soft_mix([(s_r, val_r), (s_f, fresh[pl.ds(row, span), HD : 2 * HD])])
            for h in range(HEADS):
                out[pl.ds(row - begin, span), h * HD : (h + 1) * HD] = o[h * span : (h + 1) * span]
            return carry

        lax.fori_loop(begin // span, end // span, chunk, 0)


def handed_kernel(table, lengths, all_pages, sent, out, slots, pool, sems, *, half, decode_rows, most):
    group = lax.axis_index("group")
    page_len = pool.shape[1]
    each = 4
    stack = HEADS * POS
    span = each * stack
    width = each * most * page_len

    @pl.when(group >= half)
    def _():
        out[...] = jnp.zeros_like(out)

    @pl.when(group < half)
    def _():
        def fetch(b):
            at = pl.ds(b * each * most, each * most)
            return pltpu.make_async_copy(all_pages.at[at], pool.at[at], sems.at[b])

        for b in range(half // each):
            fetch(b).start()
        for i in range(half):
            slots[table[group * half + i] // decode_rows] = group * half + i
        row_id = lax.broadcasted_iota(jnp.int32, (span, width), 0) // stack
        col = lax.broadcasted_iota(jnp.int32, (span, width), 1)
        same = col // (most * page_len) == row_id
        slot = lax.broadcasted_iota(jnp.int32, (1, width), 1)
        f_row = lax.broadcasted_iota(jnp.int32, (span, span), 0)
        f_col = lax.broadcasted_iota(jnp.int32, (span, span), 1)
        f_ok = jnp.logical_and(
            f_row // stack == f_col // stack, lax.rem(f_col, stack) <= lax.rem(f_row, POS)
        )
        for b in range(half // each):
            length = jnp.zeros((1, width), jnp.int32)
            for e in range(each):
                request = slots[b * each + e]
                length = jnp.where(slot // (most * page_len) == e, lengths[request], length)
            seen = lax.rem(slot, most * page_len) < length
            new = sent[(half // each + b) * span : (half // each + b + 1) * span, :]
            q = new[:, 0:HD]
            key_n = new[:, HD : 2 * HD]
            val_n = pltpu.roll(key_n.astype(F32), span - POS, 0).astype(BF)
            fetch(b).wait()
            own = slice(b * each * most, (b + 1) * each * most)
            key_c = pool[own, :, 0:HD].reshape(width, HD)
            val_c = pool[own, :, HD : 2 * HD].reshape(width, HD)
            s_c = jnp.where(jnp.logical_and(same, seen), nt_dot(q, key_c), NEG)
            s_n = jnp.where(f_ok, nt_dot(q, key_n), NEG)
            o = soft_mix([(s_c, val_c), (s_n, val_n)])
            for n in range(2):
                out[(n * half // each + b) * span : (n * half // each + b + 1) * span, :] = o


def front_kernel(
    table, first, second, back, weight, z_out, r_out, l_out, x_near, x_far, x13, x0, *scratch, half, decode_rows
):
    whole, held, sems, z_part, y_r, y_l, out_sems = scratch
    group = lax.axis_index("group")
    tp = lax.axis_index("tp")
    my_y, my_z = lax.rem(tp, 4), tp // 4
    cut = first.shape[0]
    rows = whole.shape[0]
    slots = half * HEADS * POS
    count, _, part = held.shape
    mid = y_r.shape[1] // part
    z_count = count - 2 * mid

    def fetch(n):
        begin = (2 * mid + n if n < z_count else n - z_count) * part
        return pltpu.make_async_copy(
            weight.at[:, pl.ds(begin, part)], held.at[n], sems.at[n]
        )

    for n in range(count):
        fetch(n).start()
    whole[0:cut] = first[...]
    whole[cut:] = second[...]

    @pl.when(group >= half)
    def _():
        want = wanted_rows(table, group, half, decode_rows)
        here = lax.broadcasted_iota(jnp.int32, (slots, rows), 1)
        put = (want == here).astype(F32).astype(BF)
        head = lax.rem(lax.broadcasted_iota(jnp.int32, (slots, HD), 0) // POS, HEADS)
        came = back[0:slots, :].astype(F32)

        def spread(x):
            return lax.dot_general(put, x, (((0,), (0,)), ((), ())), preferred_element_type=F32)

        hit = spread(jnp.ones((slots, HD), BF)) > 0.5
        for h in range(HEADS):
            at = slice(h * HD, (h + 1) * HD)
            moved = spread(jnp.where(head == h, came, 0.0).astype(BF))
            whole[:, at] = jnp.where(hit, moved, whole[:, at].astype(F32)).astype(BF)

    share = 64

    def block(dist, far):
        dest = (my_z + far - 2 * my_z * far) * 4 + lax.rem(my_y + dist, 4)
        return whole[pl.ds(pl.multiple_of(dest * share, share), share), :]

    for dist in range(4):
        x_near[dist * share : (dist + 1) * share] = block(dist, 0)
        x_far[dist * share : (dist + 1) * share] = block(dist, 1)
    for n, dist in enumerate((1, 3)):
        for far in range(2):
            x13[(2 * n + far) * share : (2 * n + far + 1) * share] = block(dist, far)
    for far in range(2):
        x0[far * share : (far + 1) * share] = block(0, far)
    x2 = jnp.concatenate([block(2, 0), block(2, 1)], axis=0)
    copies = []
    for x, begin, held_out, out in (
        (x_far[...], 0, z_part, z_out),
        (x2, z_count, y_r, r_out),
        (x2, z_count + mid, y_l, l_out),
    ):
        for n in range(held_out.shape[1] // part):
            fetch(begin + n).wait()
            held_out[:, n * part : (n + 1) * part] = nn_dot(x, held[begin + n]).astype(BF)
        copies.append(pltpu.make_async_copy(held_out, out, out_sems.at[len(copies)]))
        copies[-1].start()
    for copy in copies:
        copy.wait()


def add(*terms):
    total = terms[0].astype(F32)
    for term in terms[1:]:
        total = total + term.astype(F32)
    return total.astype(BF)


def on_device(
    queries,
    fresh_kv,
    page_pool,
    out_weight,
    request_row,
    request_len,
    request_pages,
    resident_len,
    prefix_len,
):
    half = lax.axis_size("group") // 2
    tp_count = lax.axis_size("tp")
    rows, wide = queries.shape
    kv_wide = fresh_kv.shape[1]
    pool_pages, page_len, _ = page_pool.shape
    most = request_pages.shape[1]
    decode_rows = rows // POS
    slots = half * HEADS * POS
    smem = pl.BlockSpec(memory_space=pltpu.SMEM)
    vmem = pl.BlockSpec(memory_space=pltpu.VMEM)
    hbm = pl.BlockSpec(memory_space=pltpu.HBM)
    params = pltpu.CompilerParams(vmem_limit_bytes=LIMIT * 1024 * 1024)
    less = pltpu.CompilerParams(vmem_limit_bytes=LESS * 1024 * 1024)
    dma = pltpu.SemaphoreType.DMA
    inputs = [pltpu.VMEM(queries.shape, BF), pltpu.VMEM(fresh_kv.shape, BF)]

    def made(*shape):
        return jax.ShapeDtypeStruct(shape, BF)

    def y_step(x, step):
        return lax.ppermute(x, "tp", [(t, t // 4 * 4 + (t + step) % 4) for t in range(tp_count)])

    def z_swap(x):
        return lax.ppermute(x, "tp", [(t, (t + 4) % tp_count) for t in range(tp_count)])

    table = request_row.reshape(1, half * half)
    parcel = pl.pallas_call(
        functools.partial(pick_kernel, half=half, decode_rows=decode_rows),
        out_shape=made(2 * slots, kv_wide),
        in_specs=[vmem, hbm, hbm],
        out_specs=vmem,
        scratch_shapes=[*inputs, dma((2,))],
        compiler_params=params,
        name="pick_rows",
    )(table, queries, fresh_kv)
    sent = lax.all_to_all(parcel, "group", split_axis=0, concat_axis=0, tiled=True)

    cut = FIRST * rows // 8
    by_name = request_pages.T

    def attend(part, given, specs, extra, extra_specs, scratch):
        return pl.pallas_call(
            functools.partial(
                local_kernel, half=half, decode_rows=decode_rows, part=part, cut=cut
            ),
            out_shape=[made(cut if part == 0 else rows - cut, wide), *extra],
            in_specs=[smem, smem, *specs],
            out_specs=[vmem, *extra_specs],
            scratch_shapes=[
                *inputs,
                pltpu.VMEM(page_pool.shape, BF),
                dma((2,)),
                dma((pool_pages // 8,)),
                *scratch,
            ],
            compiler_params=params,
            cost_estimate=pl.CostEstimate(
                flops=8 * 2048 * 2048 * 128, bytes_accessed=5 << 20, transcendentals=1 << 21
            ),
            name="local_attention",
        )(prefix_len, resident_len, *given)

    first, gathered = attend(
        0,
        (request_row, by_name, queries, fresh_kv, page_pool),
        [smem, smem, hbm, hbm, hbm],
        [made(half * most, page_len, kv_wide)],
        [vmem],
        [dma((half, most)), pltpu.SMEM((half,), jnp.int32)],
    )
    sent, first = lax.optimization_barrier((sent, first))
    handed = pl.pallas_call(
        functools.partial(handed_kernel, half=half, decode_rows=decode_rows, most=most),
        out_shape=made(2 * slots, HD),
        in_specs=[smem, smem, hbm, vmem],
        out_specs=vmem,
        scratch_shapes=[
            pltpu.SMEM((half,), jnp.int32),
            pltpu.VMEM((half * most, page_len, kv_wide), BF),
            dma((4,)),
        ],
        compiler_params=less,
        name="handed_attention",
    )(request_row, request_len, gathered, sent)
    back = lax.all_to_all(handed, "group", split_axis=0, concat_axis=0, tiled=True)
    (second,) = attend(1, (queries, fresh_kv, page_pool), [hbm, hbm, hbm], [], [], [])
    share = rows // tp_count
    pieces = (COLS_Y + EARLY) // PIECE
    sizes = [(4 * share, EARLY), (2 * share, COLS_Y // 2), (2 * share, COLS_Y // 2)]
    z1_a, y2_r, y2_l, x_near, x_far, x13, x0 = pl.pallas_call(
        functools.partial(front_kernel, half=half, decode_rows=decode_rows),
        out_shape=[
            *(made(*size) for size in sizes),
            made(4 * share, wide),
            made(4 * share, wide),
            made(4 * share, wide),
            made(2 * share, wide),
        ],
        in_specs=[vmem] * 4 + [hbm],
        out_specs=[hbm] * 3 + [vmem] * 4,
        scratch_shapes=[
            pltpu.VMEM((rows, wide), BF),
            pltpu.VMEM((pieces, wide, PIECE), BF),
            dma((pieces,)),
            *(pltpu.VMEM(size, BF) for size in sizes),
            dma((3,)),
        ],
        compiler_params=less,
        name="front_products",
    )(table, first, second, back, out_weight)

    def blocks(x):
        return x.reshape(-1, share, x.shape[1])

    cuts = {"y": (0, COLS_Y), "b": (COLS_Y + EARLY, None), "z": (COLS_Y, None)}

    def products(given, names):
        parts = []
        for name in names:
            begin, end = cuts[name[0]]
            weight = out_weight[:, begin:end]
            part = jnp.dot(given[name], weight, preferred_element_type=F32).astype(BF)
            part, given = lax.optimization_barrier((part, given))
            parts.append(blocks(part))
        return parts, given

    def start_far(far):
        mid = far.shape[-1] // 2
        return y_step(far[..., :mid], 1), y_step(far[..., mid:], -1)

    def start_near(next_r, next_l, far_r, far_l):
        mid = far_r.shape[-1]
        right = jnp.concatenate([add(next_r[..., :mid], far_r), next_r[..., mid:]], -1)
        left = jnp.concatenate([next_l[..., :mid], add(next_l[..., mid:], far_l)], -1)
        return y_step(right, 1), y_step(left, -1)

    come_a = z_swap(blocks(z1_a))
    far_y = y_step(blocks(y2_r), 1), y_step(blocks(y2_l), -1)
    given = {"y13": x13, "b1": x_far, "y0": x0, "z0": x_near}
    (y13, z1_b), given = products(given, ("y13", "b1"))
    far_y, come_a, z1_b, given, y13 = lax.optimization_barrier((far_y, come_a, z1_b, given, y13))
    come_b = z_swap(z1_b)
    near_y = start_near(y13[0:2], y13[2:4], *far_y)
    (y0, z0), given = products(given, ("y0", "z0"))
    near_y, come_b, y0, z0 = lax.optimization_barrier((near_y, come_b, y0, z0))
    mine_y = add(y0, *near_y)
    come_y = z_swap(mine_y[1])
    mine_z = add(z0, jnp.concatenate([come_a, come_b], axis=-1))
    far_z = start_far(mine_z[2])
    near_z = start_near(mine_z[1], mine_z[3], *far_z)
    return jnp.concatenate([add(mine_y[0], come_y), add(mine_z[0], *near_z)], axis=-1)


def solution(mesh):
    in_specs = (
        P("group", "tp"),
        P("group", "tp"),
        P("group", None, "tp"),
        P("tp", None),
        P(),
        P(),
        P(),
        P(),
        P(),
    )
    out_specs = P(("group", "tp"), None)
    return jax.shard_map(
        on_device, mesh=mesh, in_specs=in_specs, out_specs=out_specs, check_vma=False
    )
```

```python
import functools
import math

import jax
import jax.numpy as jnp
from jax import lax
from jax.experimental import pallas as pl
from jax.experimental.pallas import tpu as pltpu
from jax.sharding import PartitionSpec as P

HD = 128
POS = 4
PREF = 24
HEADS = 4
NEG = -1e30
COLS_Y = 4608
PIECE = 384
EARLY = 1152
FIRST = 4
LIMIT = 54
LESS = 52
SCALE2 = math.log2(math.e) / math.sqrt(HD)
BF = jnp.bfloat16
F32 = jnp.float32


def nt_dot(a, b):
    return lax.dot_general(a, b, (((1,), (1,)), ((), ())), preferred_element_type=F32)


def nn_dot(a, b):
    return jnp.dot(a, b, preferred_element_type=F32)


def soft_mix(pieces):
    top = functools.reduce(
        jnp.maximum, [jnp.max(s, axis=-1, keepdims=True) for s, _ in pieces]
    )
    total = 0.0
    mixed = 0.0
    for s, v in pieces:
        p = jnp.exp2((s - top) * SCALE2)
        total = total + jnp.sum(p, axis=-1, keepdims=True)
        mixed = mixed + nn_dot(p.astype(BF), v)
    return (mixed / total).astype(BF)


def wanted_rows(table, group, half, decode_rows):
    slots = half * HEADS * POS
    peer = lax.rem(group, half)
    slot = lax.broadcasted_iota(jnp.int32, (slots, half * half), 0)
    request = lax.broadcasted_iota(jnp.int32, (slots, half * half), 1)
    row = table[...]
    mine = jnp.logical_and(
        request // half == slot // (HEADS * POS), row // decode_rows == peer
    )
    first = jnp.sum(jnp.where(mine, lax.rem(row, decode_rows) * POS, 0), axis=1, keepdims=True)
    return first + lax.rem(lax.broadcasted_iota(jnp.int32, (slots, 1), 0), POS)


def load(pairs, sems):
    copies = [pltpu.make_async_copy(a, b, sems.at[n]) for n, (a, b) in enumerate(pairs)]
    for copy in copies:
        copy.start()
    return copies


def pick_kernel(table, queries, fresh, out, *, half, decode_rows):
    rows = queries.shape[0]
    slots = half * HEADS * POS
    want = wanted_rows(table, lax.axis_index("group"), half, decode_rows)
    pick = (want == lax.broadcasted_iota(jnp.int32, (slots, rows), 1)).astype(F32).astype(BF)
    head = lax.rem(lax.broadcasted_iota(jnp.int32, (slots, HD), 0) // POS, HEADS)
    got_q = nn_dot(pick, queries[...])
    got_f = nn_dot(pick, fresh[...])
    one_q = got_q[:, 0:HD]
    for h in range(1, HEADS):
        one_q = jnp.where(head == h, got_q[:, h * HD : (h + 1) * HD], one_q)
    one_f = jnp.where(head == 0, got_f[:, 0:HD], got_f[:, HD : 2 * HD])
    one_f = jnp.where(head < 2, one_f, 0.0)
    for n in range(2):
        out[n * slots : (n + 1) * slots, 0:HD] = one_q.astype(BF)
        out[n * slots : (n + 1) * slots, HD : 2 * HD] = one_f.astype(BF)


def stacked(ref, row, span):
    return jnp.concatenate(
        [ref[pl.ds(row, span), h * HD : (h + 1) * HD] for h in range(HEADS)], axis=0
    )


def fresh_mask(span):
    row = lax.rem(lax.broadcasted_iota(jnp.int32, (span * HEADS, span), 0), span)
    col = lax.broadcasted_iota(jnp.int32, (span * HEADS, span), 1)
    return jnp.logical_and(col // POS == row // POS, col <= row)


def local_kernel(
    prefix_len, resident_len, *refs, half, decode_rows, part, cut
):
    if part == 0:
        table, pages, all_q, all_f, pool, out, gathered, *scratch = refs
    else:
        all_q, all_f, pool, out, *scratch = refs
    queries, fresh, held, io_sems, sems, *more = scratch
    copies = load([(all_q, queries), (all_f, fresh)], io_sems)

    group = lax.axis_index("group")
    peer = lax.rem(group, half)
    rows = queries.shape[0]
    begin, end = (0, cut) if part == 0 else (cut, rows)
    pool_pages, page_len, _ = pool.shape
    each = 8
    parts = pool_pages // each

    def fetch(n):
        return pltpu.make_async_copy(
            pool.at[pl.ds(n * each, each)], held.at[pl.ds(n * each, each)], sems.at[n]
        )

    def side_copies():
        if part == 1:
            return []
        most = pages.shape[0]
        return [
            pltpu.make_async_copy(
                pool.at[pages[n, more[1][d]]], gathered.at[d * most + n], more[0].at[d, n]
            )
            for d in range(half)
            for n in range(most)
        ]

    @pl.when(group < half)
    def _():
        prefix_tokens = PREF * page_len
        for n in range(PREF // each):
            fetch(n).start()
        if part == 0:
            for i in range(half):
                more[1][table[group * half + i] // decode_rows] = group * half + i
        for copy in side_copies():
            copy.start()
        for copy in copies:
            copy.wait()
        for n in range(PREF // each):
            fetch(n).wait()
        prefix = prefix_len[peer]
        span = 64
        stack = span * HEADS
        ok_p = lax.broadcasted_iota(jnp.int32, (1, prefix_tokens), 1) < prefix
        row_id = lax.rem(lax.broadcasted_iota(jnp.int32, (stack, rows), 0), span)
        ahead = lax.broadcasted_iota(jnp.int32, (stack, rows), 1) - row_id

        def chunk(i, carry):
            row = pl.multiple_of(i * span, span)
            q = stacked(queries, row, span)
            key_p = held[0:PREF, :, 0:HD].reshape(prefix_tokens, HD)
            val_p = held[0:PREF, :, HD : 2 * HD].reshape(prefix_tokens, HD)
            s_p = jnp.where(ok_p, nt_dot(q, key_p), NEG)
            s_f = jnp.where(ahead <= row, nt_dot(q, fresh[:, 0:HD]), NEG)
            o = soft_mix([(s_p, val_p), (s_f, fresh[:, HD : 2 * HD])])
            for h in range(HEADS):
                out[pl.ds(row - begin, span), h * HD : (h + 1) * HD] = o[h * span : (h + 1) * span]
            return carry

        lax.fori_loop(begin // span, end // span, chunk, 0)
        for copy in side_copies():
            copy.wait()

    @pl.when(group >= half)
    def _():
        span = each * POS
        if part == 1:
            fetch(0).start()
        for n in range(begin // span, min(end // span, parts)):
            fetch(n).start()
        if part == 1:
            fetch(0).wait()
        for copy in copies:
            copy.wait()
        stack = span * HEADS
        width = each * page_len
        row_id = lax.rem(lax.broadcasted_iota(jnp.int32, (stack, width), 0), span) // POS
        col = lax.broadcasted_iota(jnp.int32, (stack, width), 1)
        same = col // page_len == row_id
        slot = lax.broadcasted_iota(jnp.int32, (1, width), 1)
        f_ok = fresh_mask(span)

        def chunk(i, carry):
            @pl.when(i < parts)
            def _():
                fetch(i).wait()

            row = pl.multiple_of(i * span, span)
            first = lax.rem(i, parts) * each
            q = stacked(queries, row, span)
            key_r = held[pl.ds(first, each), :, 0:HD].reshape(width, HD)
            val_r = held[pl.ds(first, each), :, HD : 2 * HD].reshape(width, HD)
            length = jnp.zeros((1, width), jnp.int32)
            for e in range(each):
                length = jnp.where(
                    slot // page_len == e, resident_len[peer * decode_rows + i * each + e], length
                )
            seen = lax.rem(slot, page_len) < length
            s_r = jnp.where(jnp.logical_and(same, seen), nt_dot(q, key_r), NEG)
            s_f = jnp.where(f_ok, nt_dot(q, fresh[pl.ds(row, span), 0:HD]), NEG)
            o = soft_mix([(s_r, val_r), (s_f, fresh[pl.ds(row, span), HD : 2 * HD])])
            for h in range(HEADS):
                out[pl.ds(row - begin, span), h * HD : (h + 1) * HD] = o[h * span : (h + 1) * span]
            return carry

        lax.fori_loop(begin // span, end // span, chunk, 0)


def handed_kernel(table, lengths, all_pages, sent, out, slots, pool, sems, *, half, decode_rows, most):
    group = lax.axis_index("group")
    page_len = pool.shape[1]
    each = 2
    stack = HEADS * POS
    span = each * stack
    width = each * most * page_len

    @pl.when(group >= half)
    def _():
        out[...] = jnp.zeros_like(out)

    @pl.when(group < half)
    def _():
        def fetch(b):
            at = pl.ds(b * each * most, each * most)
            return pltpu.make_async_copy(all_pages.at[at], pool.at[at], sems.at[b])

        for b in range(half // each):
            fetch(b).start()
        for i in range(half):
            slots[table[group * half + i] // decode_rows] = group * half + i
        row_id = lax.broadcasted_iota(jnp.int32, (span, width), 0) // stack
        col = lax.broadcasted_iota(jnp.int32, (span, width), 1)
        same = col // (most * page_len) == row_id
        slot = lax.broadcasted_iota(jnp.int32, (1, width), 1)
        f_row = lax.broadcasted_iota(jnp.int32, (span, span), 0)
        f_col = lax.broadcasted_iota(jnp.int32, (span, span), 1)
        f_ok = jnp.logical_and(
            f_row // stack == f_col // stack, lax.rem(f_col, stack) <= lax.rem(f_row, POS)
        )
        for b in range(half // each):
            length = jnp.zeros((1, width), jnp.int32)
            for e in range(each):
                request = slots[b * each + e]
                length = jnp.where(slot // (most * page_len) == e, lengths[request], length)
            seen = lax.rem(slot, most * page_len) < length
            new = sent[(half // each + b) * span : (half // each + b + 1) * span, :]
            q = new[:, 0:HD]
            key_n = new[:, HD : 2 * HD]
            val_n = pltpu.roll(key_n.astype(F32), span - POS, 0).astype(BF)
            fetch(b).wait()
            own = slice(b * each * most, (b + 1) * each * most)
            key_c = pool[own, :, 0:HD].reshape(width, HD)
            val_c = pool[own, :, HD : 2 * HD].reshape(width, HD)
            s_c = jnp.where(jnp.logical_and(same, seen), nt_dot(q, key_c), NEG)
            s_n = jnp.where(f_ok, nt_dot(q, key_n), NEG)
            o = soft_mix([(s_c, val_c), (s_n, val_n)])
            for n in range(2):
                out[(n * half // each + b) * span : (n * half // each + b + 1) * span, :] = o


def front_kernel(
    table, first, second, back, weight, z_out, r_out, l_out, x_near, x_far, x13, x0, *scratch, half, decode_rows
):
    whole, held, sems, z_part, y_r, y_l, out_sems = scratch
    group = lax.axis_index("group")
    tp = lax.axis_index("tp")
    my_y, my_z = lax.rem(tp, 4), tp // 4
    cut = first.shape[0]
    rows = whole.shape[0]
    slots = half * HEADS * POS
    count, _, part = held.shape
    mid = y_r.shape[1] // part
    z_count = count - 2 * mid

    def fetch(n):
        begin = (2 * mid + n if n < z_count else n - z_count) * part
        return pltpu.make_async_copy(
            weight.at[:, pl.ds(begin, part)], held.at[n], sems.at[n]
        )

    for n in range(count):
        fetch(n).start()
    whole[0:cut] = first[...]
    whole[cut:] = second[...]

    @pl.when(group >= half)
    def _():
        want = wanted_rows(table, group, half, decode_rows)
        here = lax.broadcasted_iota(jnp.int32, (slots, rows), 1)
        put = (want == here).astype(F32).astype(BF)
        head = lax.rem(lax.broadcasted_iota(jnp.int32, (slots, HD), 0) // POS, HEADS)
        came = back[0:slots, :].astype(F32)

        def spread(x):
            return lax.dot_general(put, x, (((0,), (0,)), ((), ())), preferred_element_type=F32)

        hit = spread(jnp.ones((slots, HD), BF)) > 0.5
        for h in range(HEADS):
            at = slice(h * HD, (h + 1) * HD)
            moved = spread(jnp.where(head == h, came, 0.0).astype(BF))
            whole[:, at] = jnp.where(hit, moved, whole[:, at].astype(F32)).astype(BF)

    share = 64

    def block(dist, far):
        dest = (my_z + far - 2 * my_z * far) * 4 + lax.rem(my_y + dist, 4)
        return whole[pl.ds(pl.multiple_of(dest * share, share), share), :]

    for dist in range(4):
        x_near[dist * share : (dist + 1) * share] = block(dist, 0)
        x_far[dist * share : (dist + 1) * share] = block(dist, 1)
    for n, dist in enumerate((1, 3)):
        for far in range(2):
            x13[(2 * n + far) * share : (2 * n + far + 1) * share] = block(dist, far)
    for far in range(2):
        x0[far * share : (far + 1) * share] = block(0, far)
    x2 = jnp.concatenate([block(2, 0), block(2, 1)], axis=0)
    copies = []
    for x, begin, held_out, out in (
        (x_far[...], 0, z_part, z_out),
        (x2, z_count, y_r, r_out),
        (x2, z_count + mid, y_l, l_out),
    ):
        for n in range(held_out.shape[1] // part):
            fetch(begin + n).wait()
            held_out[:, n * part : (n + 1) * part] = nn_dot(x, held[begin + n]).astype(BF)
        copies.append(pltpu.make_async_copy(held_out, out, out_sems.at[len(copies)]))
        copies[-1].start()
    for copy in copies:
        copy.wait()


def add(*terms):
    total = terms[0].astype(F32)
    for term in terms[1:]:
        total = total + term.astype(F32)
    return total.astype(BF)


def on_device(
    queries,
    fresh_kv,
    page_pool,
    out_weight,
    request_row,
    request_len,
    request_pages,
    resident_len,
    prefix_len,
):
    half = lax.axis_size("group") // 2
    tp_count = lax.axis_size("tp")
    rows, wide = queries.shape
    kv_wide = fresh_kv.shape[1]
    pool_pages, page_len, _ = page_pool.shape
    most = request_pages.shape[1]
    decode_rows = rows // POS
    slots = half * HEADS * POS
    smem = pl.BlockSpec(memory_space=pltpu.SMEM)
    vmem = pl.BlockSpec(memory_space=pltpu.VMEM)
    hbm = pl.BlockSpec(memory_space=pltpu.HBM)
    params = pltpu.CompilerParams(vmem_limit_bytes=LIMIT * 1024 * 1024)
    less = pltpu.CompilerParams(vmem_limit_bytes=LESS * 1024 * 1024)
    dma = pltpu.SemaphoreType.DMA
    inputs = [pltpu.VMEM(queries.shape, BF), pltpu.VMEM(fresh_kv.shape, BF)]

    def made(*shape):
        return jax.ShapeDtypeStruct(shape, BF)

    def y_step(x, step):
        return lax.ppermute(x, "tp", [(t, t // 4 * 4 + (t + step) % 4) for t in range(tp_count)])

    def z_swap(x):
        return lax.ppermute(x, "tp", [(t, (t + 4) % tp_count) for t in range(tp_count)])

    table = request_row.reshape(1, half * half)
    parcel = pl.pallas_call(
        functools.partial(pick_kernel, half=half, decode_rows=decode_rows),
        out_shape=made(2 * slots, kv_wide),
        in_specs=[vmem] * 3,
        out_specs=vmem,
        compiler_params=params,
        name="pick_rows",
    )(table, queries, fresh_kv)
    sent = lax.all_to_all(parcel, "group", split_axis=0, concat_axis=0, tiled=True)

    cut = FIRST * rows // 8
    by_name = request_pages.T

    def attend(part, given, specs, extra, extra_specs, scratch):
        return pl.pallas_call(
            functools.partial(
                local_kernel, half=half, decode_rows=decode_rows, part=part, cut=cut
            ),
            out_shape=[made(cut if part == 0 else rows - cut, wide), *extra],
            in_specs=[smem, smem, *specs],
            out_specs=[vmem, *extra_specs],
            scratch_shapes=[
                *inputs,
                pltpu.VMEM(page_pool.shape, BF),
                dma((2,)),
                dma((pool_pages // 8,)),
                *scratch,
            ],
            compiler_params=params,
            cost_estimate=pl.CostEstimate(
                flops=8 * 2048 * 2048 * 128, bytes_accessed=5 << 20, transcendentals=1 << 21
            ),
            name="local_attention",
        )(prefix_len, resident_len, *given)

    first, gathered = attend(
        0,
        (request_row, by_name, queries, fresh_kv, page_pool),
        [smem, smem, hbm, hbm, hbm],
        [made(half * most, page_len, kv_wide)],
        [vmem],
        [dma((half, most)), pltpu.SMEM((half,), jnp.int32)],
    )
    sent, first = lax.optimization_barrier((sent, first))
    handed = pl.pallas_call(
        functools.partial(handed_kernel, half=half, decode_rows=decode_rows, most=most),
        out_shape=made(2 * slots, HD),
        in_specs=[smem, smem, hbm, vmem],
        out_specs=vmem,
        scratch_shapes=[
            pltpu.SMEM((half,), jnp.int32),
            pltpu.VMEM((half * most, page_len, kv_wide), BF),
            dma((half // 2,)),
        ],
        compiler_params=less,
        name="handed_attention",
    )(request_row, request_len, gathered, sent)
    back = lax.all_to_all(handed, "group", split_axis=0, concat_axis=0, tiled=True)
    (second,) = attend(1, (queries, fresh_kv, page_pool), [hbm, hbm, hbm], [], [], [])
    share = rows // tp_count
    pieces = (COLS_Y + EARLY) // PIECE
    sizes = [(4 * share, EARLY), (2 * share, COLS_Y // 2), (2 * share, COLS_Y // 2)]
    z1_a, y2_r, y2_l, x_near, x_far, x13, x0 = pl.pallas_call(
        functools.partial(front_kernel, half=half, decode_rows=decode_rows),
        out_shape=[
            *(made(*size) for size in sizes),
            made(4 * share, wide),
            made(4 * share, wide),
            made(4 * share, wide),
            made(2 * share, wide),
        ],
        in_specs=[vmem] * 4 + [hbm],
        out_specs=[hbm] * 3 + [vmem] * 4,
        scratch_shapes=[
            pltpu.VMEM((rows, wide), BF),
            pltpu.VMEM((pieces, wide, PIECE), BF),
            dma((pieces,)),
            *(pltpu.VMEM(size, BF) for size in sizes),
            dma((3,)),
        ],
        compiler_params=less,
        name="front_products",
    )(table, first, second, back, out_weight)

    def blocks(x):
        return x.reshape(-1, share, x.shape[1])

    cuts = {"y": (0, COLS_Y), "b": (COLS_Y + EARLY, None), "z": (COLS_Y, None)}

    def products(given, names):
        parts = []
        for name in names:
            begin, end = cuts[name[0]]
            weight = out_weight[:, begin:end]
            part = jnp.dot(given[name], weight, preferred_element_type=F32).astype(BF)
            part, given = lax.optimization_barrier((part, given))
            parts.append(blocks(part))
        return parts, given

    def start_far(far):
        mid = far.shape[-1] // 2
        return y_step(far[..., :mid], 1), y_step(far[..., mid:], -1)

    def start_near(next_r, next_l, far_r, far_l):
        mid = far_r.shape[-1]
        right = jnp.concatenate([add(next_r[..., :mid], far_r), next_r[..., mid:]], -1)
        left = jnp.concatenate([next_l[..., :mid], add(next_l[..., mid:], far_l)], -1)
        return y_step(right, 1), y_step(left, -1)

    come_a = z_swap(blocks(z1_a))
    far_y = y_step(blocks(y2_r), 1), y_step(blocks(y2_l), -1)
    given = {"y13": x13, "b1": x_far, "y0": x0, "z0": x_near}
    (y13, z1_b), given = products(given, ("y13", "b1"))
    far_y, come_a, z1_b, given, y13 = lax.optimization_barrier((far_y, come_a, z1_b, given, y13))
    come_b = z_swap(z1_b)
    near_y = start_near(y13[0:2], y13[2:4], *far_y)
    (y0, z0), given = products(given, ("y0", "z0"))
    near_y, come_b, y0, z0 = lax.optimization_barrier((near_y, come_b, y0, z0))
    mine_y = add(y0, *near_y)
    come_y = z_swap(mine_y[1])
    mine_z = add(z0, jnp.concatenate([come_a, come_b], axis=-1))
    far_z = start_far(mine_z[2])
    near_z = start_near(mine_z[1], mine_z[3], *far_z)
    return jnp.concatenate([add(mine_y[0], come_y), add(mine_z[0], *near_z)], axis=-1)


def solution(mesh):
    in_specs = (
        P("group", "tp"),
        P("group", "tp"),
        P("group", None, "tp"),
        P("tp", None),
        P(),
        P(),
        P(),
        P(),
        P(),
    )
    out_specs = P(("group", "tp"), None)
    return jax.shard_map(
        on_device, mesh=mesh, in_specs=in_specs, out_specs=out_specs, check_vma=False
    )
```

```python
import functools
import math

import jax
import jax.numpy as jnp
from jax import lax
from jax.experimental import pallas as pl
from jax.experimental.pallas import tpu as pltpu
from jax.sharding import PartitionSpec as P

HD = 128
POS = 4
PREF = 24
HEADS = 4
NEG = -1e30
COLS_Y = 4608
PIECE = 384
EARLY = 1152
FIRST = 4
LIMIT = 54
LESS = 52
SCALE2 = math.log2(math.e) / math.sqrt(HD)
BF = jnp.bfloat16
F32 = jnp.float32


def nt_dot(a, b):
    return lax.dot_general(a, b, (((1,), (1,)), ((), ())), preferred_element_type=F32)


def nn_dot(a, b):
    return jnp.dot(a, b, preferred_element_type=F32)


def soft_mix(pieces):
    top = functools.reduce(
        jnp.maximum, [jnp.max(s, axis=-1, keepdims=True) for s, _ in pieces]
    )
    total = 0.0
    mixed = 0.0
    for s, v in pieces:
        p = jnp.exp2((s - top) * SCALE2)
        total = total + jnp.sum(p, axis=-1, keepdims=True)
        mixed = mixed + nn_dot(p.astype(BF), v)
    return (mixed / total).astype(BF)


def wanted_rows(table, group, half, decode_rows):
    slots = half * HEADS * POS
    peer = lax.rem(group, half)
    slot = lax.broadcasted_iota(jnp.int32, (slots, half * half), 0)
    request = lax.broadcasted_iota(jnp.int32, (slots, half * half), 1)
    row = table[...]
    mine = jnp.logical_and(
        request // half == slot // (HEADS * POS), row // decode_rows == peer
    )
    first = jnp.sum(jnp.where(mine, lax.rem(row, decode_rows) * POS, 0), axis=1, keepdims=True)
    return first + lax.rem(lax.broadcasted_iota(jnp.int32, (slots, 1), 0), POS)


def load(pairs, sems):
    copies = [pltpu.make_async_copy(a, b, sems.at[n]) for n, (a, b) in enumerate(pairs)]
    for copy in copies:
        copy.start()
    return copies


def pick_kernel(table, queries, fresh, out, *, half, decode_rows):
    rows = queries.shape[0]
    slots = half * HEADS * POS
    want = wanted_rows(table, lax.axis_index("group"), half, decode_rows)
    pick = (want == lax.broadcasted_iota(jnp.int32, (slots, rows), 1)).astype(F32).astype(BF)
    head = lax.rem(lax.broadcasted_iota(jnp.int32, (slots, HD), 0) // POS, HEADS)
    got_q = nn_dot(pick, queries[...])
    got_f = nn_dot(pick, fresh[...])
    one_q = got_q[:, 0:HD]
    for h in range(1, HEADS):
        one_q = jnp.where(head == h, got_q[:, h * HD : (h + 1) * HD], one_q)
    one_f = jnp.where(head == 0, got_f[:, 0:HD], got_f[:, HD : 2 * HD])
    one_f = jnp.where(head < 2, one_f, 0.0)
    for n in range(2):
        out[n * slots : (n + 1) * slots, 0:HD] = one_q.astype(BF)
        out[n * slots : (n + 1) * slots, HD : 2 * HD] = one_f.astype(BF)


def stacked(ref, row, span):
    return jnp.concatenate(
        [ref[pl.ds(row, span), h * HD : (h + 1) * HD] for h in range(HEADS)], axis=0
    )


def fresh_mask(span):
    row = lax.rem(lax.broadcasted_iota(jnp.int32, (span * HEADS, span), 0), span)
    col = lax.broadcasted_iota(jnp.int32, (span * HEADS, span), 1)
    return jnp.logical_and(col // POS == row // POS, col <= row)


def local_kernel(
    prefix_len, resident_len, *refs, half, decode_rows, part, cut
):
    if part == 0:
        table, pages, all_q, all_f, pool, out, gathered, *scratch = refs
    else:
        all_q, all_f, pool, out, *scratch = refs
    queries, fresh, held, io_sems, sems, *more = scratch
    copies = load([(all_q, queries), (all_f, fresh)], io_sems)

    group = lax.axis_index("group")
    peer = lax.rem(group, half)
    rows = queries.shape[0]
    begin, end = (0, cut) if part == 0 else (cut, rows)
    pool_pages, page_len, _ = pool.shape
    each = 8
    parts = pool_pages // each

    def fetch(n):
        return pltpu.make_async_copy(
            pool.at[pl.ds(n * each, each)], held.at[pl.ds(n * each, each)], sems.at[n]
        )

    def side_copies():
        if part == 1:
            return []
        most = pages.shape[0]
        return [
            pltpu.make_async_copy(
                pool.at[pages[n, more[1][d]]], gathered.at[d * most + n], more[0].at[d, n]
            )
            for d in range(half)
            for n in range(most)
        ]

    @pl.when(group < half)
    def _():
        prefix_tokens = PREF * page_len
        for n in range(PREF // each):
            fetch(n).start()
        if part == 0:
            for i in range(half):
                more[1][table[group * half + i] // decode_rows] = group * half + i
        for copy in side_copies():
            copy.start()
        for copy in copies:
            copy.wait()
        for n in range(PREF // each):
            fetch(n).wait()
        prefix = prefix_len[peer]
        span = 64
        stack = span * HEADS
        ok_p = lax.broadcasted_iota(jnp.int32, (1, prefix_tokens), 1) < prefix
        row_id = lax.rem(lax.broadcasted_iota(jnp.int32, (stack, rows), 0), span)
        ahead = lax.broadcasted_iota(jnp.int32, (stack, rows), 1) - row_id

        def chunk(i, carry):
            row = pl.multiple_of(i * span, span)
            q = stacked(queries, row, span)
            key_p = held[0:PREF, :, 0:HD].reshape(prefix_tokens, HD)
            val_p = held[0:PREF, :, HD : 2 * HD].reshape(prefix_tokens, HD)
            s_p = jnp.where(ok_p, nt_dot(q, key_p), NEG)
            s_f = jnp.where(ahead <= row, nt_dot(q, fresh[:, 0:HD]), NEG)
            o = soft_mix([(s_p, val_p), (s_f, fresh[:, HD : 2 * HD])])
            for h in range(HEADS):
                out[pl.ds(row - begin, span), h * HD : (h + 1) * HD] = o[h * span : (h + 1) * span]
            return carry

        lax.fori_loop(begin // span, end // span, chunk, 0)
        for copy in side_copies():
            copy.wait()

    @pl.when(group >= half)
    def _():
        span = each * POS
        if part == 1:
            fetch(0).start()
        for n in range(begin // span, min(end // span, parts)):
            fetch(n).start()
        if part == 1:
            fetch(0).wait()
        for copy in copies:
            copy.wait()
        stack = span * HEADS
        width = each * page_len
        row_id = lax.rem(lax.broadcasted_iota(jnp.int32, (stack, width), 0), span) // POS
        col = lax.broadcasted_iota(jnp.int32, (stack, width), 1)
        same = col // page_len == row_id
        slot = lax.broadcasted_iota(jnp.int32, (1, width), 1)
        f_ok = fresh_mask(span)

        def chunk(i, carry):
            @pl.when(i < parts)
            def _():
                fetch(i).wait()

            row = pl.multiple_of(i * span, span)
            first = lax.rem(i, parts) * each
            q = stacked(queries, row, span)
            key_r = held[pl.ds(first, each), :, 0:HD].reshape(width, HD)
            val_r = held[pl.ds(first, each), :, HD : 2 * HD].reshape(width, HD)
            length = jnp.zeros((1, width), jnp.int32)
            for e in range(each):
                length = jnp.where(
                    slot // page_len == e, resident_len[peer * decode_rows + i * each + e], length
                )
            seen = lax.rem(slot, page_len) < length
            s_r = jnp.where(jnp.logical_and(same, seen), nt_dot(q, key_r), NEG)
            s_f = jnp.where(f_ok, nt_dot(q, fresh[pl.ds(row, span), 0:HD]), NEG)
            o = soft_mix([(s_r, val_r), (s_f, fresh[pl.ds(row, span), HD : 2 * HD])])
            for h in range(HEADS):
                out[pl.ds(row - begin, span), h * HD : (h + 1) * HD] = o[h * span : (h + 1) * span]
            return carry

        lax.fori_loop(begin // span, end // span, chunk, 0)


def handed_kernel(table, lengths, all_pages, sent, out, slots, pool, sems, *, half, decode_rows, most):
    group = lax.axis_index("group")
    page_len = pool.shape[1]
    each = 4
    stack = HEADS * POS
    span = each * stack
    width = each * most * page_len

    @pl.when(group >= half)
    def _():
        out[...] = jnp.zeros_like(out)

    @pl.when(group < half)
    def _():
        def fetch(b):
            at = pl.ds(b * each * most, each * most)
            return pltpu.make_async_copy(all_pages.at[at], pool.at[at], sems.at[b])

        for b in range(half // each):
            fetch(b).start()
        for i in range(half):
            slots[table[group * half + i] // decode_rows] = group * half + i
        row_id = lax.broadcasted_iota(jnp.int32, (span, width), 0) // stack
        col = lax.broadcasted_iota(jnp.int32, (span, width), 1)
        same = col // (most * page_len) == row_id
        slot = lax.broadcasted_iota(jnp.int32, (1, width), 1)
        f_row = lax.broadcasted_iota(jnp.int32, (span, span), 0)
        f_col = lax.broadcasted_iota(jnp.int32, (span, span), 1)
        f_ok = jnp.logical_and(
            f_row // stack == f_col // stack, lax.rem(f_col, stack) <= lax.rem(f_row, POS)
        )
        for b in range(half // each):
            length = jnp.zeros((1, width), jnp.int32)
            for e in range(each):
                request = slots[b * each + e]
                length = jnp.where(slot // (most * page_len) == e, lengths[request], length)
            seen = lax.rem(slot, most * page_len) < length
            new = sent[(half // each + b) * span : (half // each + b + 1) * span, :]
            q = new[:, 0:HD]
            key_n = new[:, HD : 2 * HD]
            val_n = pltpu.roll(key_n.astype(F32), span - POS, 0).astype(BF)
            fetch(b).wait()
            own = slice(b * each * most, (b + 1) * each * most)
            key_c = pool[own, :, 0:HD].reshape(width, HD)
            val_c = pool[own, :, HD : 2 * HD].reshape(width, HD)
            s_c = jnp.where(jnp.logical_and(same, seen), nt_dot(q, key_c), NEG)
            s_n = jnp.where(f_ok, nt_dot(q, key_n), NEG)
            o = soft_mix([(s_c, val_c), (s_n, val_n)])
            for n in range(2):
                out[(n * half // each + b) * span : (n * half // each + b + 1) * span, :] = o


def front_kernel(
    table, first, second, back, weight, z_out, y_outs, x_near, x_far, x13, x0, *scratch, half, decode_rows
):
    whole, held, sems, z_part, y_parts, out_sems = scratch
    group = lax.axis_index("group")
    tp = lax.axis_index("tp")
    my_y, my_z = lax.rem(tp, 4), tp // 4
    cut = first.shape[0]
    rows = whole.shape[0]
    slots = half * HEADS * POS
    count, _, part = held.shape
    quarter = y_parts[0].shape[1] // part
    z_count = count - 4 * quarter

    def fetch(n):
        begin = (4 * quarter + n if n < z_count else n - z_count) * part
        return pltpu.make_async_copy(
            weight.at[:, pl.ds(begin, part)], held.at[n], sems.at[n]
        )

    for n in range(count):
        fetch(n).start()
    whole[0:cut] = first[...]
    whole[cut:] = second[...]

    @pl.when(group >= half)
    def _():
        want = wanted_rows(table, group, half, decode_rows)
        here = lax.broadcasted_iota(jnp.int32, (slots, rows), 1)
        put = (want == here).astype(F32).astype(BF)
        head = lax.rem(lax.broadcasted_iota(jnp.int32, (slots, HD), 0) // POS, HEADS)
        came = back[0:slots, :].astype(F32)

        def spread(x):
            return lax.dot_general(put, x, (((0,), (0,)), ((), ())), preferred_element_type=F32)

        hit = spread(jnp.ones((slots, HD), BF)) > 0.5
        for h in range(HEADS):
            at = slice(h * HD, (h + 1) * HD)
            moved = spread(jnp.where(head == h, came, 0.0).astype(BF))
            whole[:, at] = jnp.where(hit, moved, whole[:, at].astype(F32)).astype(BF)

    share = 64

    def block(dist, far):
        dest = (my_z + far - 2 * my_z * far) * 4 + lax.rem(my_y + dist, 4)
        return whole[pl.ds(pl.multiple_of(dest * share, share), share), :]

    for dist in range(4):
        x_near[dist * share : (dist + 1) * share] = block(dist, 0)
        x_far[dist * share : (dist + 1) * share] = block(dist, 1)
    for n, dist in enumerate((1, 3)):
        for far in range(2):
            x13[(2 * n + far) * share : (2 * n + far + 1) * share] = block(dist, far)
    for far in range(2):
        x0[far * share : (far + 1) * share] = block(0, far)
    x2 = jnp.concatenate([block(2, 0), block(2, 1)], axis=0)
    copies = []
    order = [(x2, z_count + i * quarter, y_parts[i], y_outs[i]) for i in range(4)]
    order.insert(0, (x_far[...], 0, z_part, z_out))
    for x, begin, held_out, out in order:
        for n in range(held_out.shape[1] // part):
            fetch(begin + n).wait()
            held_out[:, n * part : (n + 1) * part] = nn_dot(x, held[begin + n]).astype(BF)
        copies.append(pltpu.make_async_copy(held_out, out, out_sems.at[len(copies)]))
        copies[-1].start()
    for copy in copies:
        copy.wait()


def add(*terms):
    total = terms[0].astype(F32)
    for term in terms[1:]:
        total = total + term.astype(F32)
    return total.astype(BF)


def on_device(
    queries,
    fresh_kv,
    page_pool,
    out_weight,
    request_row,
    request_len,
    request_pages,
    resident_len,
    prefix_len,
):
    half = lax.axis_size("group") // 2
    tp_count = lax.axis_size("tp")
    rows, wide = queries.shape
    kv_wide = fresh_kv.shape[1]
    pool_pages, page_len, _ = page_pool.shape
    most = request_pages.shape[1]
    decode_rows = rows // POS
    slots = half * HEADS * POS
    smem = pl.BlockSpec(memory_space=pltpu.SMEM)
    vmem = pl.BlockSpec(memory_space=pltpu.VMEM)
    hbm = pl.BlockSpec(memory_space=pltpu.HBM)
    params = pltpu.CompilerParams(vmem_limit_bytes=LIMIT * 1024 * 1024)
    less = pltpu.CompilerParams(vmem_limit_bytes=LESS * 1024 * 1024)
    dma = pltpu.SemaphoreType.DMA
    inputs = [pltpu.VMEM(queries.shape, BF), pltpu.VMEM(fresh_kv.shape, BF)]

    def made(*shape):
        return jax.ShapeDtypeStruct(shape, BF)

    def y_step(x, step):
        return lax.ppermute(x, "tp", [(t, t // 4 * 4 + (t + step) % 4) for t in range(tp_count)])

    def z_swap(x):
        return lax.ppermute(x, "tp", [(t, (t + 4) % tp_count) for t in range(tp_count)])

    table = request_row.reshape(1, half * half)
    parcel = pl.pallas_call(
        functools.partial(pick_kernel, half=half, decode_rows=decode_rows),
        out_shape=made(2 * slots, kv_wide),
        in_specs=[vmem] * 3,
        out_specs=vmem,
        compiler_params=params,
        name="pick_rows",
    )(table, queries, fresh_kv)
    sent = lax.all_to_all(parcel, "group", split_axis=0, concat_axis=0, tiled=True)

    cut = FIRST * rows // 8
    by_name = request_pages.T

    def attend(part, given, specs, extra, extra_specs, scratch):
        return pl.pallas_call(
            functools.partial(
                local_kernel, half=half, decode_rows=decode_rows, part=part, cut=cut
            ),
            out_shape=[made(cut if part == 0 else rows - cut, wide), *extra],
            in_specs=[smem, smem, *specs],
            out_specs=[vmem, *extra_specs],
            scratch_shapes=[
                *inputs,
                pltpu.VMEM(page_pool.shape, BF),
                dma((2,)),
                dma((pool_pages // 8,)),
                *scratch,
            ],
            compiler_params=params,
            cost_estimate=pl.CostEstimate(
                flops=8 * 2048 * 2048 * 128, bytes_accessed=5 << 20, transcendentals=1 << 21
            ),
            name="local_attention",
        )(prefix_len, resident_len, *given)

    first, gathered = attend(
        0,
        (request_row, by_name, queries, fresh_kv, page_pool),
        [smem, smem, hbm, hbm, hbm],
        [made(half * most, page_len, kv_wide)],
        [vmem],
        [dma((half, most)), pltpu.SMEM((half,), jnp.int32)],
    )
    sent, first = lax.optimization_barrier((sent, first))
    handed = pl.pallas_call(
        functools.partial(handed_kernel, half=half, decode_rows=decode_rows, most=most),
        out_shape=made(2 * slots, HD),
        in_specs=[smem, smem, hbm, vmem],
        out_specs=vmem,
        scratch_shapes=[
            pltpu.SMEM((half,), jnp.int32),
            pltpu.VMEM((half * most, page_len, kv_wide), BF),
            dma((half // 4,)),
        ],
        compiler_params=less,
        name="handed_attention",
    )(request_row, request_len, gathered, sent)
    back = lax.all_to_all(handed, "group", split_axis=0, concat_axis=0, tiled=True)
    (second,) = attend(1, (queries, fresh_kv, page_pool), [hbm, hbm, hbm], [], [], [])
    share = rows // tp_count
    pieces = (COLS_Y + EARLY) // PIECE
    quarter = (2 * share, COLS_Y // 4)
    z1_a, y2, x_near, x_far, x13, x0 = pl.pallas_call(
        functools.partial(front_kernel, half=half, decode_rows=decode_rows),
        out_shape=[
            made(4 * share, EARLY),
            [made(*quarter)] * 4,
            made(4 * share, wide),
            made(4 * share, wide),
            made(4 * share, wide),
            made(2 * share, wide),
        ],
        in_specs=[vmem] * 4 + [hbm],
        out_specs=[hbm, [hbm] * 4] + [vmem] * 4,
        scratch_shapes=[
            pltpu.VMEM((rows, wide), BF),
            pltpu.VMEM((pieces, wide, PIECE), BF),
            dma((pieces,)),
            pltpu.VMEM((4 * share, EARLY), BF),
            [pltpu.VMEM(quarter, BF)] * 4,
            dma((5,)),
        ],
        compiler_params=less,
        name="front_products",
    )(table, first, second, back, out_weight)

    def blocks(x):
        return x.reshape(-1, share, x.shape[1])

    cuts = {
        "p": (0, COLS_Y // 2),
        "q": (COLS_Y // 2, COLS_Y),
        "y": (0, COLS_Y),
        "b": (COLS_Y + EARLY, None),
        "z": (COLS_Y, None),
    }

    def products(given, names):
        parts = []
        for name in names:
            begin, end = cuts[name[0]]
            weight = out_weight[:, begin:end]
            part = jnp.dot(given[name], weight, preferred_element_type=F32).astype(BF)
            part, given = lax.optimization_barrier((part, given))
            parts.append(blocks(part))
        return parts, given

    def start_far(far):
        mid = far.shape[-1] // 2
        return y_step(far[..., :mid], 1), y_step(far[..., mid:], -1)

    def start_near(next_r, next_l, far_r, far_l):
        mid = far_r.shape[-1]
        right = jnp.concatenate([add(next_r[..., :mid], far_r), next_r[..., mid:]], -1)
        left = jnp.concatenate([next_l[..., :mid], add(next_l[..., mid:], far_l)], -1)
        return y_step(right, 1), y_step(left, -1)

    far_p = y_step(blocks(y2[0]), 1), y_step(blocks(y2[1]), -1)
    come_a = z_swap(blocks(z1_a))
    given = {"p13": x13, "b1": x_far, "q13": x13, "y0": x0, "z0": x_near}
    (p13,), given = products(given, ("p13",))
    p13, q_r, q_l = lax.optimization_barrier((p13, y2[2], y2[3]))
    far_q = y_step(blocks(q_r), 1), y_step(blocks(q_l), -1)
    (z1_b,), given = products(given, ("b1",))
    far_p, p13, z1_b, given = lax.optimization_barrier((far_p, p13, z1_b, given))
    near_p = start_near(p13[0:2], p13[2:4], *far_p)
    come_a, far_q, z1_b, given = lax.optimization_barrier((come_a, far_q, z1_b, given))
    come_b = z_swap(z1_b)
    (q13,), given = products(given, ("q13",))
    near_q = start_near(q13[0:2], q13[2:4], *far_q)
    (y0, z0), given = products(given, ("y0", "z0"))
    near_p, near_q, come_b, y0, z0 = lax.optimization_barrier((near_p, near_q, come_b, y0, z0))
    mid = COLS_Y // 2
    mine_y = jnp.concatenate(
        [add(y0[..., :mid], *near_p), add(y0[..., mid:], *near_q)], axis=-1
    )
    come_y = z_swap(mine_y[1])
    mine_z = add(z0, jnp.concatenate([come_a, come_b], axis=-1))
    far_z = start_far(mine_z[2])
    near_z = start_near(mine_z[1], mine_z[3], *far_z)
    return jnp.concatenate([add(mine_y[0], come_y), add(mine_z[0], *near_z)], axis=-1)


def solution(mesh):
    in_specs = (
        P("group", "tp"),
        P("group", "tp"),
        P("group", None, "tp"),
        P("tp", None),
        P(),
        P(),
        P(),
        P(),
        P(),
    )
    out_specs = P(("group", "tp"), None)
    return jax.shard_map(
        on_device, mesh=mesh, in_specs=in_specs, out_specs=out_specs, check_vma=False
    )
```

```python
import functools
import math

import jax
import jax.numpy as jnp
from jax import lax
from jax.experimental import pallas as pl
from jax.experimental.pallas import tpu as pltpu
from jax.sharding import PartitionSpec as P

HD = 128
POS = 4
PREF = 24
HEADS = 4
NEG = -1e30
COLS_Y = 4608
PIECE = 384
EARLY = 1536
FIRST = 4
LIMIT = 54
LESS = 52
SCALE2 = math.log2(math.e) / math.sqrt(HD)
BF = jnp.bfloat16
F32 = jnp.float32


def nt_dot(a, b):
    return lax.dot_general(a, b, (((1,), (1,)), ((), ())), preferred_element_type=F32)


def nn_dot(a, b):
    return jnp.dot(a, b, preferred_element_type=F32)


def soft_mix(pieces):
    top = functools.reduce(
        jnp.maximum, [jnp.max(s, axis=-1, keepdims=True) for s, _ in pieces]
    )
    total = 0.0
    mixed = 0.0
    for s, v in pieces:
        p = jnp.exp2((s - top) * SCALE2)
        total = total + jnp.sum(p, axis=-1, keepdims=True)
        mixed = mixed + nn_dot(p.astype(BF), v)
    return (mixed / total).astype(BF)


def wanted_rows(table, group, half, decode_rows):
    slots = half * HEADS * POS
    peer = lax.rem(group, half)
    slot = lax.broadcasted_iota(jnp.int32, (slots, half * half), 0)
    request = lax.broadcasted_iota(jnp.int32, (slots, half * half), 1)
    row = table[...]
    mine = jnp.logical_and(
        request // half == slot // (HEADS * POS), row // decode_rows == peer
    )
    first = jnp.sum(jnp.where(mine, lax.rem(row, decode_rows) * POS, 0), axis=1, keepdims=True)
    return first + lax.rem(lax.broadcasted_iota(jnp.int32, (slots, 1), 0), POS)


def load(pairs, sems):
    copies = [pltpu.make_async_copy(a, b, sems.at[n]) for n, (a, b) in enumerate(pairs)]
    for copy in copies:
        copy.start()
    return copies


def pick_kernel(table, queries, fresh, out, *, half, decode_rows):
    rows = queries.shape[0]
    slots = half * HEADS * POS
    want = wanted_rows(table, lax.axis_index("group"), half, decode_rows)
    pick = (want == lax.broadcasted_iota(jnp.int32, (slots, rows), 1)).astype(F32).astype(BF)
    head = lax.rem(lax.broadcasted_iota(jnp.int32, (slots, HD), 0) // POS, HEADS)
    got_q = nn_dot(pick, queries[...])
    got_f = nn_dot(pick, fresh[...])
    one_q = got_q[:, 0:HD]
    for h in range(1, HEADS):
        one_q = jnp.where(head == h, got_q[:, h * HD : (h + 1) * HD], one_q)
    one_f = jnp.where(head == 0, got_f[:, 0:HD], got_f[:, HD : 2 * HD])
    one_f = jnp.where(head < 2, one_f, 0.0)
    for n in range(2):
        out[n * slots : (n + 1) * slots, 0:HD] = one_q.astype(BF)
        out[n * slots : (n + 1) * slots, HD : 2 * HD] = one_f.astype(BF)


def stacked(ref, row, span):
    return jnp.concatenate(
        [ref[pl.ds(row, span), h * HD : (h + 1) * HD] for h in range(HEADS)], axis=0
    )


def fresh_mask(span):
    row = lax.rem(lax.broadcasted_iota(jnp.int32, (span * HEADS, span), 0), span)
    col = lax.broadcasted_iota(jnp.int32, (span * HEADS, span), 1)
    return jnp.logical_and(col // POS == row // POS, col <= row)


def local_kernel(
    prefix_len, resident_len, *refs, half, decode_rows, part, cut
):
    if part == 0:
        table, pages, all_q, all_f, pool, out, gathered, *scratch = refs
    else:
        all_q, all_f, pool, out, *scratch = refs
    queries, fresh, held, io_sems, sems, *more = scratch
    copies = load([(all_q, queries), (all_f, fresh)], io_sems)

    group = lax.axis_index("group")
    peer = lax.rem(group, half)
    rows = queries.shape[0]
    begin, end = (0, cut) if part == 0 else (cut, rows)
    pool_pages, page_len, _ = pool.shape
    each = 8
    parts = pool_pages // each

    def fetch(n):
        return pltpu.make_async_copy(
            pool.at[pl.ds(n * each, each)], held.at[pl.ds(n * each, each)], sems.at[n]
        )

    def side_copies():
        if part == 1:
            return []
        most = pages.shape[0]
        return [
            pltpu.make_async_copy(
                pool.at[pages[n, more[1][d]]], gathered.at[d * most + n], more[0].at[d, n]
            )
            for d in range(half)
            for n in range(most)
        ]

    @pl.when(group < half)
    def _():
        prefix_tokens = PREF * page_len
        for n in range(PREF // each):
            fetch(n).start()
        if part == 0:
            for i in range(half):
                more[1][table[group * half + i] // decode_rows] = group * half + i
        for copy in side_copies():
            copy.start()
        for copy in copies:
            copy.wait()
        for n in range(PREF // each):
            fetch(n).wait()
        prefix = prefix_len[peer]
        span = 64
        stack = span * HEADS
        ok_p = lax.broadcasted_iota(jnp.int32, (1, prefix_tokens), 1) < prefix
        row_id = lax.rem(lax.broadcasted_iota(jnp.int32, (stack, rows), 0), span)
        ahead = lax.broadcasted_iota(jnp.int32, (stack, rows), 1) - row_id

        def chunk(i, carry):
            row = pl.multiple_of(i * span, span)
            q = stacked(queries, row, span)
            key_p = held[0:PREF, :, 0:HD].reshape(prefix_tokens, HD)
            val_p = held[0:PREF, :, HD : 2 * HD].reshape(prefix_tokens, HD)
            s_p = jnp.where(ok_p, nt_dot(q, key_p), NEG)
            s_f = jnp.where(ahead <= row, nt_dot(q, fresh[:, 0:HD]), NEG)
            o = soft_mix([(s_p, val_p), (s_f, fresh[:, HD : 2 * HD])])
            for h in range(HEADS):
                out[pl.ds(row - begin, span), h * HD : (h + 1) * HD] = o[h * span : (h + 1) * span]
            return carry

        lax.fori_loop(begin // span, end // span, chunk, 0)
        for copy in side_copies():
            copy.wait()

    @pl.when(group >= half)
    def _():
        span = each * POS
        if part == 1:
            fetch(0).start()
        for n in range(begin // span, min(end // span, parts)):
            fetch(n).start()
        if part == 1:
            fetch(0).wait()
        for copy in copies:
            copy.wait()
        stack = span * HEADS
        width = each * page_len
        row_id = lax.rem(lax.broadcasted_iota(jnp.int32, (stack, width), 0), span) // POS
        col = lax.broadcasted_iota(jnp.int32, (stack, width), 1)
        same = col // page_len == row_id
        slot = lax.broadcasted_iota(jnp.int32, (1, width), 1)
        f_ok = fresh_mask(span)

        def chunk(i, carry):
            @pl.when(i < parts)
            def _():
                fetch(i).wait()

            row = pl.multiple_of(i * span, span)
            first = lax.rem(i, parts) * each
            q = stacked(queries, row, span)
            key_r = held[pl.ds(first, each), :, 0:HD].reshape(width, HD)
            val_r = held[pl.ds(first, each), :, HD : 2 * HD].reshape(width, HD)
            length = jnp.zeros((1, width), jnp.int32)
            for e in range(each):
                length = jnp.where(
                    slot // page_len == e, resident_len[peer * decode_rows + i * each + e], length
                )
            seen = lax.rem(slot, page_len) < length
            s_r = jnp.where(jnp.logical_and(same, seen), nt_dot(q, key_r), NEG)
            s_f = jnp.where(f_ok, nt_dot(q, fresh[pl.ds(row, span), 0:HD]), NEG)
            o = soft_mix([(s_r, val_r), (s_f, fresh[pl.ds(row, span), HD : 2 * HD])])
            for h in range(HEADS):
                out[pl.ds(row - begin, span), h * HD : (h + 1) * HD] = o[h * span : (h + 1) * span]
            return carry

        lax.fori_loop(begin // span, end // span, chunk, 0)


def handed_kernel(table, lengths, all_pages, sent, out, slots, pool, sems, *, half, decode_rows, most):
    group = lax.axis_index("group")
    page_len = pool.shape[1]
    each = 4
    stack = HEADS * POS
    span = each * stack
    width = each * most * page_len

    @pl.when(group >= half)
    def _():
        out[...] = jnp.zeros_like(out)

    @pl.when(group < half)
    def _():
        def fetch(b):
            at = pl.ds(b * each * most, each * most)
            return pltpu.make_async_copy(all_pages.at[at], pool.at[at], sems.at[b])

        for b in range(half // each):
            fetch(b).start()
        for i in range(half):
            slots[table[group * half + i] // decode_rows] = group * half + i
        row_id = lax.broadcasted_iota(jnp.int32, (span, width), 0) // stack
        col = lax.broadcasted_iota(jnp.int32, (span, width), 1)
        same = col // (most * page_len) == row_id
        slot = lax.broadcasted_iota(jnp.int32, (1, width), 1)
        f_row = lax.broadcasted_iota(jnp.int32, (span, span), 0)
        f_col = lax.broadcasted_iota(jnp.int32, (span, span), 1)
        f_ok = jnp.logical_and(
            f_row // stack == f_col // stack, lax.rem(f_col, stack) <= lax.rem(f_row, POS)
        )
        for b in range(half // each):
            length = jnp.zeros((1, width), jnp.int32)
            for e in range(each):
                request = slots[b * each + e]
                length = jnp.where(slot // (most * page_len) == e, lengths[request], length)
            seen = lax.rem(slot, most * page_len) < length
            new = sent[(half // each + b) * span : (half // each + b + 1) * span, :]
            q = new[:, 0:HD]
            key_n = new[:, HD : 2 * HD]
            val_n = pltpu.roll(key_n.astype(F32), span - POS, 0).astype(BF)
            fetch(b).wait()
            own = slice(b * each * most, (b + 1) * each * most)
            key_c = pool[own, :, 0:HD].reshape(width, HD)
            val_c = pool[own, :, HD : 2 * HD].reshape(width, HD)
            s_c = jnp.where(jnp.logical_and(same, seen), nt_dot(q, key_c), NEG)
            s_n = jnp.where(f_ok, nt_dot(q, key_n), NEG)
            o = soft_mix([(s_c, val_c), (s_n, val_n)])
            for n in range(2):
                out[(n * half // each + b) * span : (n * half // each + b + 1) * span, :] = o


def front_kernel(
    table, first, second, back, weight, z_out, y_outs, x_near, x_far, x13, x0, *scratch, half, decode_rows
):
    whole, held, sems, z_part, y_parts, out_sems = scratch
    group = lax.axis_index("group")
    tp = lax.axis_index("tp")
    my_y, my_z = lax.rem(tp, 4), tp // 4
    cut = first.shape[0]
    rows = whole.shape[0]
    slots = half * HEADS * POS
    count, _, part = held.shape
    quarter = y_parts[0].shape[1] // part
    z_count = count - 4 * quarter

    def fetch(n):
        begin = (4 * quarter + n if n < z_count else n - z_count) * part
        return pltpu.make_async_copy(
            weight.at[:, pl.ds(begin, part)], held.at[n], sems.at[n]
        )

    for n in range(count):
        fetch(n).start()
    whole[0:cut] = first[...]
    whole[cut:] = second[...]

    @pl.when(group >= half)
    def _():
        want = wanted_rows(table, group, half, decode_rows)
        here = lax.broadcasted_iota(jnp.int32, (slots, rows), 1)
        put = (want == here).astype(F32).astype(BF)
        head = lax.rem(lax.broadcasted_iota(jnp.int32, (slots, HD), 0) // POS, HEADS)
        came = back[0:slots, :].astype(F32)

        def spread(x):
            return lax.dot_general(put, x, (((0,), (0,)), ((), ())), preferred_element_type=F32)

        hit = spread(jnp.ones((slots, HD), BF)) > 0.5
        for h in range(HEADS):
            at = slice(h * HD, (h + 1) * HD)
            moved = spread(jnp.where(head == h, came, 0.0).astype(BF))
            whole[:, at] = jnp.where(hit, moved, whole[:, at].astype(F32)).astype(BF)

    share = 64

    def block(dist, far):
        dest = (my_z + far - 2 * my_z * far) * 4 + lax.rem(my_y + dist, 4)
        return whole[pl.ds(pl.multiple_of(dest * share, share), share), :]

    for dist in range(4):
        x_near[dist * share : (dist + 1) * share] = block(dist, 0)
        x_far[dist * share : (dist + 1) * share] = block(dist, 1)
    for n, dist in enumerate((1, 3)):
        for far in range(2):
            x13[(2 * n + far) * share : (2 * n + far + 1) * share] = block(dist, far)
    for far in range(2):
        x0[far * share : (far + 1) * share] = block(0, far)
    x2 = jnp.concatenate([block(2, 0), block(2, 1)], axis=0)
    copies = []
    order = [(x2, z_count + i * quarter, y_parts[i], y_outs[i]) for i in range(4)]
    order.insert(0, (x_far[...], 0, z_part, z_out))
    for x, begin, held_out, out in order:
        for n in range(held_out.shape[1] // part):
            fetch(begin + n).wait()
            held_out[:, n * part : (n + 1) * part] = nn_dot(x, held[begin + n]).astype(BF)
        copies.append(pltpu.make_async_copy(held_out, out, out_sems.at[len(copies)]))
        copies[-1].start()
    for copy in copies:
        copy.wait()


def add(*terms):
    total = terms[0].astype(F32)
    for term in terms[1:]:
        total = total + term.astype(F32)
    return total.astype(BF)


def on_device(
    queries,
    fresh_kv,
    page_pool,
    out_weight,
    request_row,
    request_len,
    request_pages,
    resident_len,
    prefix_len,
):
    half = lax.axis_size("group") // 2
    tp_count = lax.axis_size("tp")
    rows, wide = queries.shape
    kv_wide = fresh_kv.shape[1]
    pool_pages, page_len, _ = page_pool.shape
    most = request_pages.shape[1]
    decode_rows = rows // POS
    slots = half * HEADS * POS
    smem = pl.BlockSpec(memory_space=pltpu.SMEM)
    vmem = pl.BlockSpec(memory_space=pltpu.VMEM)
    hbm = pl.BlockSpec(memory_space=pltpu.HBM)
    params = pltpu.CompilerParams(vmem_limit_bytes=LIMIT * 1024 * 1024)
    less = pltpu.CompilerParams(vmem_limit_bytes=LESS * 1024 * 1024)
    dma = pltpu.SemaphoreType.DMA
    inputs = [pltpu.VMEM(queries.shape, BF), pltpu.VMEM(fresh_kv.shape, BF)]

    def made(*shape):
        return jax.ShapeDtypeStruct(shape, BF)

    def y_step(x, step):
        return lax.ppermute(x, "tp", [(t, t // 4 * 4 + (t + step) % 4) for t in range(tp_count)])

    def z_swap(x):
        return lax.ppermute(x, "tp", [(t, (t + 4) % tp_count) for t in range(tp_count)])

    table = request_row.reshape(1, half * half)
    parcel = pl.pallas_call(
        functools.partial(pick_kernel, half=half, decode_rows=decode_rows),
        out_shape=made(2 * slots, kv_wide),
        in_specs=[vmem] * 3,
        out_specs=vmem,
        compiler_params=params,
        name="pick_rows",
    )(table, queries, fresh_kv)
    sent = lax.all_to_all(parcel, "group", split_axis=0, concat_axis=0, tiled=True)

    cut = FIRST * rows // 8
    by_name = request_pages.T

    def attend(part, given, specs, extra, extra_specs, scratch):
        return pl.pallas_call(
            functools.partial(
                local_kernel, half=half, decode_rows=decode_rows, part=part, cut=cut
            ),
            out_shape=[made(cut if part == 0 else rows - cut, wide), *extra],
            in_specs=[smem, smem, *specs],
            out_specs=[vmem, *extra_specs],
            scratch_shapes=[
                *inputs,
                pltpu.VMEM(page_pool.shape, BF),
                dma((2,)),
                dma((pool_pages // 8,)),
                *scratch,
            ],
            compiler_params=params,
            cost_estimate=pl.CostEstimate(
                flops=8 * 2048 * 2048 * 128, bytes_accessed=5 << 20, transcendentals=1 << 21
            ),
            name="local_attention",
        )(prefix_len, resident_len, *given)

    first, gathered = attend(
        0,
        (request_row, by_name, queries, fresh_kv, page_pool),
        [smem, smem, hbm, hbm, hbm],
        [made(half * most, page_len, kv_wide)],
        [vmem],
        [dma((half, most)), pltpu.SMEM((half,), jnp.int32)],
    )
    sent, first = lax.optimization_barrier((sent, first))
    handed = pl.pallas_call(
        functools.partial(handed_kernel, half=half, decode_rows=decode_rows, most=most),
        out_shape=made(2 * slots, HD),
        in_specs=[smem, smem, hbm, vmem],
        out_specs=vmem,
        scratch_shapes=[
            pltpu.SMEM((half,), jnp.int32),
            pltpu.VMEM((half * most, page_len, kv_wide), BF),
            dma((half // 4,)),
        ],
        compiler_params=less,
        name="handed_attention",
    )(request_row, request_len, gathered, sent)
    back = lax.all_to_all(handed, "group", split_axis=0, concat_axis=0, tiled=True)
    (second,) = attend(1, (queries, fresh_kv, page_pool), [hbm, hbm, hbm], [], [], [])
    share = rows // tp_count
    pieces = (COLS_Y + EARLY) // PIECE
    quarter = (2 * share, COLS_Y // 4)
    z1_a, y2, x_near, x_far, x13, x0 = pl.pallas_call(
        functools.partial(front_kernel, half=half, decode_rows=decode_rows),
        out_shape=[
            made(4 * share, EARLY),
            [made(*quarter)] * 4,
            made(4 * share, wide),
            made(4 * share, wide),
            made(4 * share, wide),
            made(2 * share, wide),
        ],
        in_specs=[vmem] * 4 + [hbm],
        out_specs=[hbm, [hbm] * 4] + [vmem] * 4,
        scratch_shapes=[
            pltpu.VMEM((rows, wide), BF),
            pltpu.VMEM((pieces, wide, PIECE), BF),
            dma((pieces,)),
            pltpu.VMEM((4 * share, EARLY), BF),
            [pltpu.VMEM(quarter, BF)] * 4,
            dma((5,)),
        ],
        compiler_params=less,
        name="front_products",
    )(table, first, second, back, out_weight)

    def blocks(x):
        return x.reshape(-1, share, x.shape[1])

    cuts = {
        "p": (0, COLS_Y // 2),
        "q": (COLS_Y // 2, COLS_Y),
        "y": (0, COLS_Y),
        "b": (COLS_Y + EARLY, None),
        "z": (COLS_Y, None),
    }

    def products(given, names):
        parts = []
        for name in names:
            begin, end = cuts[name[0]]
            weight = out_weight[:, begin:end]
            part = jnp.dot(given[name], weight, preferred_element_type=F32).astype(BF)
            part, given = lax.optimization_barrier((part, given))
            parts.append(blocks(part))
        return parts, given

    def start_far(far):
        mid = far.shape[-1] // 2
        return y_step(far[..., :mid], 1), y_step(far[..., mid:], -1)

    def start_near(next_r, next_l, far_r, far_l):
        mid = far_r.shape[-1]
        right = jnp.concatenate([add(next_r[..., :mid], far_r), next_r[..., mid:]], -1)
        left = jnp.concatenate([next_l[..., :mid], add(next_l[..., mid:], far_l)], -1)
        return y_step(right, 1), y_step(left, -1)

    far_p = y_step(blocks(y2[0]), 1), y_step(blocks(y2[1]), -1)
    come_a = z_swap(blocks(z1_a))
    given = {"p13": x13, "b1": x_far, "q13": x13, "y0": x0, "z0": x_near}
    (p13,), given = products(given, ("p13",))
    p13, q_r, q_l = lax.optimization_barrier((p13, y2[2], y2[3]))
    far_q = y_step(blocks(q_r), 1), y_step(blocks(q_l), -1)
    (z1_b,), given = products(given, ("b1",))
    far_p, p13, z1_b, given = lax.optimization_barrier((far_p, p13, z1_b, given))
    near_p = start_near(p13[0:2], p13[2:4], *far_p)
    come_a, far_q, z1_b, given = lax.optimization_barrier((come_a, far_q, z1_b, given))
    come_b = z_swap(z1_b)
    (q13,), given = products(given, ("q13",))
    near_q = start_near(q13[0:2], q13[2:4], *far_q)
    (y0, z0), given = products(given, ("y0", "z0"))
    near_p, near_q, come_b, y0, z0 = lax.optimization_barrier((near_p, near_q, come_b, y0, z0))
    mid = COLS_Y // 2
    mine_y = jnp.concatenate(
        [add(y0[..., :mid], *near_p), add(y0[..., mid:], *near_q)], axis=-1
    )
    come_y = z_swap(mine_y[1])
    mine_z = add(z0, jnp.concatenate([come_a, come_b], axis=-1))
    far_z = start_far(mine_z[2])
    near_z = start_near(mine_z[1], mine_z[3], *far_z)
    return jnp.concatenate([add(mine_y[0], come_y), add(mine_z[0], *near_z)], axis=-1)


def solution(mesh):
    in_specs = (
        P("group", "tp"),
        P("group", "tp"),
        P("group", None, "tp"),
        P("tp", None),
        P(),
        P(),
        P(),
        P(),
        P(),
    )
    out_specs = P(("group", "tp"), None)
    return jax.shard_map(
        on_device, mesh=mesh, in_specs=in_specs, out_specs=out_specs, check_vma=False
    )
```

```python
import functools
import math

import jax
import jax.numpy as jnp
from jax import lax
from jax.experimental import pallas as pl
from jax.experimental.pallas import tpu as pltpu
from jax.sharding import PartitionSpec as P

HD = 128
POS = 4
PREF = 24
HEADS = 4
NEG = -1e30
COLS_Y = 4608
PIECE = 384
EARLY = 1536
FIRST = 4
LIMIT = 54
LESS = 52
SCALE2 = math.log2(math.e) / math.sqrt(HD)
BF = jnp.bfloat16
F32 = jnp.float32


def nt_dot(a, b):
    return lax.dot_general(a, b, (((1,), (1,)), ((), ())), preferred_element_type=F32)


def nn_dot(a, b):
    return jnp.dot(a, b, preferred_element_type=F32)


def soft_mix(pieces):
    top = functools.reduce(
        jnp.maximum, [jnp.max(s, axis=-1, keepdims=True) for s, _ in pieces]
    )
    total = 0.0
    mixed = 0.0
    for s, v in pieces:
        p = jnp.exp2((s - top) * SCALE2)
        total = total + jnp.sum(p, axis=-1, keepdims=True)
        mixed = mixed + nn_dot(p.astype(BF), v)
    return (mixed / total).astype(BF)


def wanted_rows(table, group, half, decode_rows):
    slots = half * HEADS * POS
    peer = lax.rem(group, half)
    slot = lax.broadcasted_iota(jnp.int32, (slots, half * half), 0)
    request = lax.broadcasted_iota(jnp.int32, (slots, half * half), 1)
    row = table[...]
    mine = jnp.logical_and(
        request // half == slot // (HEADS * POS), row // decode_rows == peer
    )
    first = jnp.sum(jnp.where(mine, lax.rem(row, decode_rows) * POS, 0), axis=1, keepdims=True)
    return first + lax.rem(lax.broadcasted_iota(jnp.int32, (slots, 1), 0), POS)


def load(pairs, sems):
    copies = [pltpu.make_async_copy(a, b, sems.at[n]) for n, (a, b) in enumerate(pairs)]
    for copy in copies:
        copy.start()
    return copies


def pick_kernel(table, queries, fresh, out, *, half, decode_rows):
    rows = queries.shape[0]
    slots = half * HEADS * POS
    want = wanted_rows(table, lax.axis_index("group"), half, decode_rows)
    pick = (want == lax.broadcasted_iota(jnp.int32, (slots, rows), 1)).astype(F32).astype(BF)
    head = lax.rem(lax.broadcasted_iota(jnp.int32, (slots, HD), 0) // POS, HEADS)
    got_q = nn_dot(pick, queries[...])
    got_f = nn_dot(pick, fresh[...])
    one_q = got_q[:, 0:HD]
    for h in range(1, HEADS):
        one_q = jnp.where(head == h, got_q[:, h * HD : (h + 1) * HD], one_q)
    one_f = jnp.where(head == 0, got_f[:, 0:HD], got_f[:, HD : 2 * HD])
    one_f = jnp.where(head < 2, one_f, 0.0)
    for n in range(2):
        out[n * slots : (n + 1) * slots, 0:HD] = one_q.astype(BF)
        out[n * slots : (n + 1) * slots, HD : 2 * HD] = one_f.astype(BF)


def stacked(ref, row, span):
    return jnp.concatenate(
        [ref[pl.ds(row, span), h * HD : (h + 1) * HD] for h in range(HEADS)], axis=0
    )


def fresh_mask(span):
    row = lax.rem(lax.broadcasted_iota(jnp.int32, (span * HEADS, span), 0), span)
    col = lax.broadcasted_iota(jnp.int32, (span * HEADS, span), 1)
    return jnp.logical_and(col // POS == row // POS, col <= row)


def local_kernel(
    prefix_len, resident_len, *refs, half, decode_rows, part, cut
):
    if part == 0:
        table, pages, all_q, all_f, pool, out, gathered, *scratch = refs
    else:
        all_q, all_f, pool, out, *scratch = refs
    queries, fresh, held, io_sems, sems, *more = scratch
    copies = load([(all_q, queries), (all_f, fresh)], io_sems)

    group = lax.axis_index("group")
    peer = lax.rem(group, half)
    rows = queries.shape[0]
    begin, end = (0, cut) if part == 0 else (cut, rows)
    pool_pages, page_len, _ = pool.shape
    each = 8
    parts = pool_pages // each

    def fetch(n):
        return pltpu.make_async_copy(
            pool.at[pl.ds(n * each, each)], held.at[pl.ds(n * each, each)], sems.at[n]
        )

    def side_copies():
        if part == 1:
            return []
        most = pages.shape[0]
        return [
            pltpu.make_async_copy(
                pool.at[pages[n, more[1][d]]], gathered.at[d * most + n], more[0].at[d, n]
            )
            for d in range(half)
            for n in range(most)
        ]

    @pl.when(group < half)
    def _():
        prefix_tokens = PREF * page_len
        for n in range(PREF // each):
            fetch(n).start()
        if part == 0:
            for i in range(half):
                more[1][table[group * half + i] // decode_rows] = group * half + i
        for copy in side_copies():
            copy.start()
        for copy in copies:
            copy.wait()
        for n in range(PREF // each):
            fetch(n).wait()
        prefix = prefix_len[peer]
        span = 64
        stack = span * HEADS
        ok_p = lax.broadcasted_iota(jnp.int32, (1, prefix_tokens), 1) < prefix
        row_id = lax.rem(lax.broadcasted_iota(jnp.int32, (stack, rows), 0), span)
        ahead = lax.broadcasted_iota(jnp.int32, (stack, rows), 1) - row_id

        def chunk(i, carry):
            row = pl.multiple_of(i * span, span)
            q = stacked(queries, row, span)
            key_p = held[0:PREF, :, 0:HD].reshape(prefix_tokens, HD)
            val_p = held[0:PREF, :, HD : 2 * HD].reshape(prefix_tokens, HD)
            s_p = jnp.where(ok_p, nt_dot(q, key_p), NEG)
            s_f = jnp.where(ahead <= row, nt_dot(q, fresh[:, 0:HD]), NEG)
            o = soft_mix([(s_p, val_p), (s_f, fresh[:, HD : 2 * HD])])
            for h in range(HEADS):
                out[pl.ds(row - begin, span), h * HD : (h + 1) * HD] = o[h * span : (h + 1) * span]
            return carry

        lax.fori_loop(begin // span, end // span, chunk, 0)
        for copy in side_copies():
            copy.wait()

    @pl.when(group >= half)
    def _():
        span = each * POS
        if part == 1:
            fetch(0).start()
        for n in range(begin // span, min(end // span, parts)):
            fetch(n).start()
        if part == 1:
            fetch(0).wait()
        for copy in copies:
            copy.wait()
        stack = span * HEADS
        width = each * page_len
        row_id = lax.rem(lax.broadcasted_iota(jnp.int32, (stack, width), 0), span) // POS
        col = lax.broadcasted_iota(jnp.int32, (stack, width), 1)
        same = col // page_len == row_id
        slot = lax.broadcasted_iota(jnp.int32, (1, width), 1)
        f_ok = fresh_mask(span)

        def chunk(i, carry):
            @pl.when(i < parts)
            def _():
                fetch(i).wait()

            row = pl.multiple_of(i * span, span)
            first = lax.rem(i, parts) * each
            q = stacked(queries, row, span)
            key_r = held[pl.ds(first, each), :, 0:HD].reshape(width, HD)
            val_r = held[pl.ds(first, each), :, HD : 2 * HD].reshape(width, HD)
            length = jnp.zeros((1, width), jnp.int32)
            for e in range(each):
                length = jnp.where(
                    slot // page_len == e, resident_len[peer * decode_rows + i * each + e], length
                )
            seen = lax.rem(slot, page_len) < length
            s_r = jnp.where(jnp.logical_and(same, seen), nt_dot(q, key_r), NEG)
            s_f = jnp.where(f_ok, nt_dot(q, fresh[pl.ds(row, span), 0:HD]), NEG)
            o = soft_mix([(s_r, val_r), (s_f, fresh[pl.ds(row, span), HD : 2 * HD])])
            for h in range(HEADS):
                out[pl.ds(row - begin, span), h * HD : (h + 1) * HD] = o[h * span : (h + 1) * span]
            return carry

        lax.fori_loop(begin // span, end // span, chunk, 0)


def handed_kernel(table, lengths, all_pages, sent, out, slots, pool, sems, *, half, decode_rows, most):
    group = lax.axis_index("group")
    page_len = pool.shape[1]
    each = 4
    stack = HEADS * POS
    span = each * stack
    width = each * most * page_len

    @pl.when(group >= half)
    def _():
        out[...] = jnp.zeros_like(out)

    @pl.when(group < half)
    def _():
        def fetch(b):
            at = pl.ds(b * each * most, each * most)
            return pltpu.make_async_copy(all_pages.at[at], pool.at[at], sems.at[b])

        for b in range(half // each):
            fetch(b).start()
        for i in range(half):
            slots[table[group * half + i] // decode_rows] = group * half + i
        row_id = lax.broadcasted_iota(jnp.int32, (span, width), 0) // stack
        col = lax.broadcasted_iota(jnp.int32, (span, width), 1)
        same = col // (most * page_len) == row_id
        slot = lax.broadcasted_iota(jnp.int32, (1, width), 1)
        f_row = lax.broadcasted_iota(jnp.int32, (span, span), 0)
        f_col = lax.broadcasted_iota(jnp.int32, (span, span), 1)
        f_ok = jnp.logical_and(
            f_row // stack == f_col // stack, lax.rem(f_col, stack) <= lax.rem(f_row, POS)
        )
        for b in range(half // each):
            fetch(b).wait()
        for b in range(half // each):
            length = jnp.zeros((1, width), jnp.int32)
            for e in range(each):
                request = slots[b * each + e]
                length = jnp.where(slot // (most * page_len) == e, lengths[request], length)
            seen = lax.rem(slot, most * page_len) < length
            new = sent[(half // each + b) * span : (half // each + b + 1) * span, :]
            q = new[:, 0:HD]
            key_n = new[:, HD : 2 * HD]
            val_n = pltpu.roll(key_n.astype(F32), span - POS, 0).astype(BF)
            own = slice(b * each * most, (b + 1) * each * most)
            key_c = pool[own, :, 0:HD].reshape(width, HD)
            val_c = pool[own, :, HD : 2 * HD].reshape(width, HD)
            s_c = jnp.where(jnp.logical_and(same, seen), nt_dot(q, key_c), NEG)
            s_n = jnp.where(f_ok, nt_dot(q, key_n), NEG)
            o = soft_mix([(s_c, val_c), (s_n, val_n)])
            for n in range(2):
                out[(n * half // each + b) * span : (n * half // each + b + 1) * span, :] = o


def front_kernel(
    table, first, second, back, weight, z_out, y_outs, x_near, x_far, x13, x0, *scratch, half, decode_rows
):
    whole, held, sems, z_part, y_parts, out_sems = scratch
    group = lax.axis_index("group")
    tp = lax.axis_index("tp")
    my_y, my_z = lax.rem(tp, 4), tp // 4
    cut = first.shape[0]
    rows = whole.shape[0]
    slots = half * HEADS * POS
    count, _, part = held.shape
    quarter = y_parts[0].shape[1] // part
    z_count = count - 4 * quarter

    def fetch(n):
        begin = (4 * quarter + n if n < z_count else n - z_count) * part
        return pltpu.make_async_copy(
            weight.at[:, pl.ds(begin, part)], held.at[n], sems.at[n]
        )

    for n in range(count):
        fetch(n).start()
    whole[0:cut] = first[...]
    whole[cut:] = second[...]

    @pl.when(group >= half)
    def _():
        want = wanted_rows(table, group, half, decode_rows)
        here = lax.broadcasted_iota(jnp.int32, (slots, rows), 1)
        put = (want == here).astype(F32).astype(BF)
        head = lax.rem(lax.broadcasted_iota(jnp.int32, (slots, HD), 0) // POS, HEADS)
        came = back[0:slots, :].astype(F32)

        def spread(x):
            return lax.dot_general(put, x, (((0,), (0,)), ((), ())), preferred_element_type=F32)

        hit = spread(jnp.ones((slots, HD), BF)) > 0.5
        for h in range(HEADS):
            at = slice(h * HD, (h + 1) * HD)
            moved = spread(jnp.where(head == h, came, 0.0).astype(BF))
            whole[:, at] = jnp.where(hit, moved, whole[:, at].astype(F32)).astype(BF)

    share = 64

    def block(dist, far):
        dest = (my_z + far - 2 * my_z * far) * 4 + lax.rem(my_y + dist, 4)
        return whole[pl.ds(pl.multiple_of(dest * share, share), share), :]

    for dist in range(4):
        x_near[dist * share : (dist + 1) * share] = block(dist, 0)
        x_far[dist * share : (dist + 1) * share] = block(dist, 1)
    for n, dist in enumerate((1, 3)):
        for far in range(2):
            x13[(2 * n + far) * share : (2 * n + far + 1) * share] = block(dist, far)
    for far in range(2):
        x0[far * share : (far + 1) * share] = block(0, far)
    x2 = jnp.concatenate([block(2, 0), block(2, 1)], axis=0)
    copies = []
    order = [(x2, z_count + i * quarter, y_parts[i], y_outs[i]) for i in range(4)]
    order.insert(0, (x_far[...], 0, z_part, z_out))
    for x, begin, held_out, out in order:
        for n in range(held_out.shape[1] // part):
            fetch(begin + n).wait()
            held_out[:, n * part : (n + 1) * part] = nn_dot(x, held[begin + n]).astype(BF)
        copies.append(pltpu.make_async_copy(held_out, out, out_sems.at[len(copies)]))
        copies[-1].start()
    for copy in copies:
        copy.wait()


def add(*terms):
    total = terms[0].astype(F32)
    for term in terms[1:]:
        total = total + term.astype(F32)
    return total.astype(BF)


def on_device(
    queries,
    fresh_kv,
    page_pool,
    out_weight,
    request_row,
    request_len,
    request_pages,
    resident_len,
    prefix_len,
):
    half = lax.axis_size("group") // 2
    tp_count = lax.axis_size("tp")
    rows, wide = queries.shape
    kv_wide = fresh_kv.shape[1]
    pool_pages, page_len, _ = page_pool.shape
    most = request_pages.shape[1]
    decode_rows = rows // POS
    slots = half * HEADS * POS
    smem = pl.BlockSpec(memory_space=pltpu.SMEM)
    vmem = pl.BlockSpec(memory_space=pltpu.VMEM)
    hbm = pl.BlockSpec(memory_space=pltpu.HBM)
    params = pltpu.CompilerParams(vmem_limit_bytes=LIMIT * 1024 * 1024)
    less = pltpu.CompilerParams(vmem_limit_bytes=LESS * 1024 * 1024)
    dma = pltpu.SemaphoreType.DMA
    inputs = [pltpu.VMEM(queries.shape, BF), pltpu.VMEM(fresh_kv.shape, BF)]

    def made(*shape):
        return jax.ShapeDtypeStruct(shape, BF)

    def y_step(x, step):
        return lax.ppermute(x, "tp", [(t, t // 4 * 4 + (t + step) % 4) for t in range(tp_count)])

    def z_swap(x):
        return lax.ppermute(x, "tp", [(t, (t + 4) % tp_count) for t in range(tp_count)])

    table = request_row.reshape(1, half * half)
    parcel = pl.pallas_call(
        functools.partial(pick_kernel, half=half, decode_rows=decode_rows),
        out_shape=made(2 * slots, kv_wide),
        in_specs=[vmem] * 3,
        out_specs=vmem,
        compiler_params=params,
        name="pick_rows",
    )(table, queries, fresh_kv)
    sent = lax.all_to_all(parcel, "group", split_axis=0, concat_axis=0, tiled=True)

    cut = FIRST * rows // 8
    by_name = request_pages.T

    def attend(part, given, specs, extra, extra_specs, scratch):
        return pl.pallas_call(
            functools.partial(
                local_kernel, half=half, decode_rows=decode_rows, part=part, cut=cut
            ),
            out_shape=[made(cut if part == 0 else rows - cut, wide), *extra],
            in_specs=[smem, smem, *specs],
            out_specs=[vmem, *extra_specs],
            scratch_shapes=[
                *inputs,
                pltpu.VMEM(page_pool.shape, BF),
                dma((2,)),
                dma((pool_pages // 8,)),
                *scratch,
            ],
            compiler_params=params,
            cost_estimate=pl.CostEstimate(
                flops=8 * 2048 * 2048 * 128, bytes_accessed=5 << 20, transcendentals=1 << 21
            ),
            name="local_attention",
        )(prefix_len, resident_len, *given)

    first, gathered = attend(
        0,
        (request_row, by_name, queries, fresh_kv, page_pool),
        [smem, smem, hbm, hbm, hbm],
        [made(half * most, page_len, kv_wide)],
        [vmem],
        [dma((half, most)), pltpu.SMEM((half,), jnp.int32)],
    )
    sent, first = lax.optimization_barrier((sent, first))
    handed = pl.pallas_call(
        functools.partial(handed_kernel, half=half, decode_rows=decode_rows, most=most),
        out_shape=made(2 * slots, HD),
        in_specs=[smem, smem, hbm, vmem],
        out_specs=vmem,
        scratch_shapes=[
            pltpu.SMEM((half,), jnp.int32),
            pltpu.VMEM((half * most, page_len, kv_wide), BF),
            dma((half // 4,)),
        ],
        compiler_params=less,
        name="handed_attention",
    )(request_row, request_len, gathered, sent)
    back = lax.all_to_all(handed, "group", split_axis=0, concat_axis=0, tiled=True)
    (second,) = attend(1, (queries, fresh_kv, page_pool), [hbm, hbm, hbm], [], [], [])
    share = rows // tp_count
    pieces = (COLS_Y + EARLY) // PIECE
    quarter = (2 * share, COLS_Y // 4)
    z1_a, y2, x_near, x_far, x13, x0 = pl.pallas_call(
        functools.partial(front_kernel, half=half, decode_rows=decode_rows),
        out_shape=[
            made(4 * share, EARLY),
            [made(*quarter)] * 4,
            made(4 * share, wide),
            made(4 * share, wide),
            made(4 * share, wide),
            made(2 * share, wide),
        ],
        in_specs=[vmem] * 4 + [hbm],
        out_specs=[hbm, [hbm] * 4] + [vmem] * 4,
        scratch_shapes=[
            pltpu.VMEM((rows, wide), BF),
            pltpu.VMEM((pieces, wide, PIECE), BF),
            dma((pieces,)),
            pltpu.VMEM((4 * share, EARLY), BF),
            [pltpu.VMEM(quarter, BF)] * 4,
            dma((5,)),
        ],
        compiler_params=params,
        name="front_products",
    )(table, first, second, back, out_weight)

    def blocks(x):
        return x.reshape(-1, share, x.shape[1])

    cuts = {
        "p": (0, COLS_Y // 2),
        "q": (COLS_Y // 2, COLS_Y),
        "y": (0, COLS_Y),
        "b": (COLS_Y + EARLY, None),
        "z": (COLS_Y, None),
    }

    def products(given, names):
        parts = []
        for name in names:
            begin, end = cuts[name[0]]
            weight = out_weight[:, begin:end]
            part = jnp.dot(given[name], weight, preferred_element_type=F32).astype(BF)
            part, given = lax.optimization_barrier((part, given))
            parts.append(blocks(part))
        return parts, given

    def start_far(far):
        mid = far.shape[-1] // 2
        return y_step(far[..., :mid], 1), y_step(far[..., mid:], -1)

    def start_near(next_r, next_l, far_r, far_l):
        mid = far_r.shape[-1]
        right = jnp.concatenate([add(next_r[..., :mid], far_r), next_r[..., mid:]], -1)
        left = jnp.concatenate([next_l[..., :mid], add(next_l[..., mid:], far_l)], -1)
        return y_step(right, 1), y_step(left, -1)

    far_p = y_step(blocks(y2[0]), 1), y_step(blocks(y2[1]), -1)
    come_a = z_swap(blocks(z1_a))
    given = {"p13": x13, "b1": x_far, "q13": x13, "y0": x0, "z0": x_near}
    (p13,), given = products(given, ("p13",))
    p13, q_r, q_l = lax.optimization_barrier((p13, y2[2], y2[3]))
    far_q = y_step(blocks(q_r), 1), y_step(blocks(q_l), -1)
    (z1_b,), given = products(given, ("b1",))
    far_p, p13, z1_b, given = lax.optimization_barrier((far_p, p13, z1_b, given))
    near_p = start_near(p13[0:2], p13[2:4], *far_p)
    come_a, far_q, z1_b, given = lax.optimization_barrier((come_a, far_q, z1_b, given))
    come_b = z_swap(z1_b)
    (q13,), given = products(given, ("q13",))
    near_q = start_near(q13[0:2], q13[2:4], *far_q)
    (y0, z0), given = products(given, ("y0", "z0"))
    near_p, near_q, come_b, y0, z0 = lax.optimization_barrier((near_p, near_q, come_b, y0, z0))
    mid = COLS_Y // 2
    mine_y = jnp.concatenate(
        [add(y0[..., :mid], *near_p), add(y0[..., mid:], *near_q)], axis=-1
    )
    come_y = z_swap(mine_y[1])
    mine_z = add(z0, jnp.concatenate([come_a, come_b], axis=-1))
    far_z = start_far(mine_z[2])
    near_z = start_near(mine_z[1], mine_z[3], *far_z)
    return jnp.concatenate([add(mine_y[0], come_y), add(mine_z[0], *near_z)], axis=-1)


def solution(mesh):
    in_specs = (
        P("group", "tp"),
        P("group", "tp"),
        P("group", None, "tp"),
        P("tp", None),
        P(),
        P(),
        P(),
        P(),
        P(),
    )
    out_specs = P(("group", "tp"), None)
    return jax.shard_map(
        on_device, mesh=mesh, in_specs=in_specs, out_specs=out_specs, check_vma=False
    )
```
